32 devices in a mesh: groups: 2 (over y), leaf: 4 (over z), sub: 2 (over x), rep: 2 (over core).
Axes of the slice: x: 2, y: 2, z: 4, core: 2. Of those that a mesh axis runs over, the one named last changes fastest.
Arguments:
- coords: float32 [3, 32, 8, 256], P(None, ('groups', 'leaf'), 'sub'), parts along dimension 1, may hold values from 0 to 16, as said below
- vector: float32 [8, 32, 8, 256], P('rep', ('groups', 'leaf'), 'sub'), parts along dimension 1, may hold values from -6 to 6
Outputs:
- potential: float32 [8, 32, 8, 256], P('rep', ('groups', 'leaf'), 'sub'), parts along dimension 1
The draws below stay inside these ranges and needn't reach their ends.
There are 2 independent parts, one for each index of `groups`. The reference program is written for one: setup_inputs(seed, part) draws one part's arguments, and reference() takes and returns one part's arrays. A program takes and returns all parts, laid end to end along the dimension named above; each array names one. Nothing has to cross between parts.
Inputs may be any that keep to these rules, and one draw needn't show every extreme that they name: `coords`: point a of leaf box (i, j) has its first coordinate in [i, i + 1), its second in [j, j + 1) and its third in [0, 1).
All inputs are finite; a program needn't handle non-finite values.
Results may differ from the reference program's by a relative error of at most 0.0003.
Values sent between devices are 32-bit elements; how exact they have to be, the bound alone decides.
A program may use at most 64 MiB of HBM per device.

```python
import jax
import jax.numpy as jnp
import numpy as np
from jax import lax

PTS = 256
COLS = 8
GX = 16
GY = 8


def draw_coords(key, part):
    key = jax.random.fold_in(key, 11)
    uniform_draw = jax.random.uniform(key, (3, GX, GY, PTS), jnp.float32)
    inside = 0.01 + 0.98 * uniform_draw
    row_shift = jnp.arange(GX, dtype=jnp.float32)[:, None, None]
    col_shift = jnp.arange(GY, dtype=jnp.float32)[None, :, None]
    return jnp.stack([inside[0] + row_shift, inside[1] + col_shift, inside[2]], 0)


def steps_of(rng, extent, pieces, smallest, top_value):
    level, own = 1.0, jax.random.fold_in(rng, 6)
    for position, parts in pieces:
        draws = jnp.exp(jax.random.uniform(jax.random.fold_in(own, position), (parts,), jnp.float32, smallest / len(pieces), top_value / len(pieces)))
        level = level * jnp.repeat(draws, extent[position] // parts).reshape([-1 if axis == position else 1 for axis in range(len(extent))])
    return level


def bell_draw(rng, shape, width, bound, cuts=(), kind=jnp.bfloat16):
    drawn = width * jax.random.normal(rng, shape, jnp.float32)
    if cuts:
        drawn = drawn * steps_of(rng, shape, cuts, -0.22, 0.18)
    return jnp.clip(drawn, -bound, bound).astype(kind)


def setup_inputs(seed: int = 0, part: int = 0) -> dict:
    arg_keys = jax.random.split(jax.random.key(seed), 3)
    part_keys = jax.random.split(jax.random.fold_in(arg_keys[2], part), 3)
    return {
        "coords": draw_coords(jax.random.fold_in(jax.random.fold_in(arg_keys[2], part), 71), part),
        "vector": bell_draw(part_keys[1], (COLS, GX, GY, PTS), 1.0, 6.0, ((0, 2), (1, 4), (2, 2)), jnp.float32),
    }


QUAD_WEIGHT = 1.0 / 64.0
SMOOTHING = 0.01
HIGHEST = lax.Precision.HIGHEST
CHEB_NODES = np.cos((2.0 * np.arange(4) + 1.0) * np.pi / 8.0)

def poly_values(points):
    second = 2.0 * points * points - 1.0
    third = 2.0 * points * second - points
    return (points, second, third)

def cheb_numpy(values):
    nodes_one, nodes_two, nodes_three = poly_values(CHEB_NODES)
    first, second, third = poly_values(values)
    return 0.25 + 0.5 * (first[..., None] * nodes_one + second[..., None] * nodes_two + third[..., None] * nodes_three)

def chebyshev(values):
    nodes_one, nodes_two, nodes_three = poly_values(CHEB_NODES)
    first, second, third = poly_values(values)
    return 0.25 + 0.5 * (first[..., None] * jnp.asarray(nodes_one, jnp.float32) + second[..., None] * jnp.asarray(nodes_two, jnp.float32) + third[..., None] * jnp.asarray(nodes_three, jnp.float32))

def transfer_table():
    halves = [cheb_numpy((CHEB_NODES + 2.0 * side_bit - 1.0) / 2.0) for side_bit in range(2)]
    same_node = np.eye(4)
    blocks = [[(halves[row_bit][:, None, None, :, None, None] * halves[col_bit][None, :, None, None, :, None] * same_node[None, None, :, None, None, :]).reshape(64, 64) for col_bit in range(2)] for row_bit in range(2)]
    return np.array(blocks)

def couple_table(tree_level):
    box_width = 2.0 ** tree_level
    across = 0.5 * box_width * CHEB_NODES
    height = 0.5 + 0.5 * CHEB_NODES
    target = np.stack(np.meshgrid(across, across, height, indexing='ij'), -1).reshape(64, 3)
    table_rows = []
    for row_shift in range(-3, 4):
        table_line = []
        for col_shift in range(-3, 4):
            source = target + np.array([row_shift * box_width, col_shift * box_width, 0.0])
            spacing = target[:, None, :] - source[None, :, :]
            values = QUAD_WEIGHT / np.sqrt(np.sum(spacing * spacing, -1) + SMOOTHING)
            far_flag = float(max(abs(row_shift), abs(col_shift)) >= 2)
            table_line.append(values * far_flag)
        table_rows.append(table_line)
    return np.array(table_rows)

def near_leaf(target, source):
    squares = jnp.zeros((source.shape[1], source.shape[2], target.shape[1]), jnp.float32)
    for axis_id in range(3):
        spacing = source[axis_id][:, :, None] - target[axis_id][None, None, :]
        squares = squares + spacing * spacing
    kernel = QUAD_WEIGHT * lax.rsqrt(squares + SMOOTHING)
    return jnp.einsum('cnb,nba->ca', source[3:], kernel, precision=HIGHEST)

def near_block(padded):
    stack_depth = padded.shape[0]
    rows_here = padded.shape[1] - 2
    cols_here = padded.shape[2] - 2
    point_count = padded.shape[3]
    pair_rows = cols_here // 2
    zero_index = jnp.zeros((), jnp.int32)

    def per_pair(pair_id):
        row_at = (pair_id // pair_rows).astype(jnp.int32)
        col_at = (2 * (pair_id % pair_rows)).astype(jnp.int32)
        window = lax.dynamic_slice(padded, (zero_index, row_at, col_at, zero_index), (stack_depth, 3, 4, point_count))
        targets = jnp.stack([window[:3, 1, 1], window[:3, 1, 2]])
        sources = jnp.stack([jnp.stack([window[:, row_shift, col_shift + offset] for row_shift in range(3) for col_shift in range(3)], 1) for offset in range(2)])
        return jax.vmap(near_leaf)(targets, sources)
    result = lax.map(per_pair, jnp.arange(rows_here * pair_rows, dtype=jnp.int32))
    result = result.reshape(rows_here, cols_here, stack_depth - 3, point_count)
    return jnp.transpose(result, (2, 0, 1, 3))

def leaf_basis(coords, start_row, start_col):
    rows_here = coords.shape[1]
    cols_here = coords.shape[2]
    row_mid = (start_row + jnp.arange(rows_here, dtype=jnp.int32)).astype(jnp.float32)[:, None, None] + 0.5
    col_mid = (start_col + jnp.arange(cols_here, dtype=jnp.int32)).astype(jnp.float32)[None, :, None] + 0.5
    along_x = jnp.moveaxis(chebyshev(2.0 * (coords[0] - row_mid)), -1, 2)
    along_y = jnp.moveaxis(chebyshev(2.0 * (coords[1] - col_mid)), -1, 2)
    along_z = jnp.moveaxis(chebyshev(2.0 * coords[2] - 1.0), -1, 2)
    product = along_x[:, :, :, None, None, :] * along_y[:, :, None, :, None, :] * along_z[:, :, None, None, :, :]
    return product.reshape(rows_here, cols_here, 64, coords.shape[3])

def make_moments(basis_table, vector):
    return jnp.einsum('ijra,cija->ijcr', basis_table, vector, precision=HIGHEST)

def evaluate_far(basis_table, summed):
    return jnp.einsum('ijra,ijcr->cija', basis_table, summed, precision=HIGHEST)

def upward(moments):
    rows_here, cols_here, column_count = (moments.shape[0], moments.shape[1], moments.shape[2])
    blocks = moments.reshape(rows_here // 2, 2, cols_here // 2, 2, column_count, 64)
    table = jnp.asarray(transfer_table(), jnp.float32)
    return jnp.einsum('idjecs,desr->ijcr', blocks, table, precision=HIGHEST)

def downward(parent_local):
    rows_here, cols_here, column_count = (parent_local.shape[0], parent_local.shape[1], parent_local.shape[2])
    table = jnp.asarray(transfer_table(), jnp.float32)
    children = jnp.einsum('ijcr,desr->idjecs', parent_local, table, precision=HIGHEST)
    return children.reshape(2 * rows_here, 2 * cols_here, column_count, 64)

def coupling_block(window, start_row, start_col, tree_level):
    rows_here = window.shape[0] - 6
    cols_here = window.shape[1] - 6
    offsets = jnp.arange(7, dtype=jnp.int32) - 3
    row_ids = (start_row + jnp.arange(rows_here, dtype=jnp.int32)).astype(jnp.int32)
    col_ids = (start_col + jnp.arange(cols_here, dtype=jnp.int32)).astype(jnp.int32)
    row_ok = jnp.abs(jnp.floor_divide(row_ids[None, :] + offsets[:, None], 2) - jnp.floor_divide(row_ids, 2)[None, :]) <= 1
    col_ok = jnp.abs(jnp.floor_divide(col_ids[None, :] + offsets[:, None], 2) - jnp.floor_divide(col_ids, 2)[None, :]) <= 1
    table = jnp.asarray(couple_table(tree_level), jnp.float32)
    total = jnp.zeros((rows_here, cols_here, window.shape[2], 64), jnp.float32)
    for row_shift in range(7):
        slab = jnp.stack([window[row_shift:row_shift + rows_here, col_shift:col_shift + cols_here] for col_shift in range(7)])
        weight = (row_ok[row_shift][None, :, None] & col_ok[:, None, :]).astype(jnp.float32)
        total = total + jnp.einsum('vxycs,vrs->xycr', slab * weight[:, :, :, None, None], table[row_shift], precision=HIGHEST)
    return total

def reference(coords, vector):
    grid_cols = coords.shape[2]
    top_level = grid_cols.bit_length() - 1
    padded = jnp.pad(jnp.concatenate([coords, vector], 0), ((0, 0), (1, 1), (1, 1), (0, 0)))
    near_part = near_block(padded)
    basis_table = leaf_basis(coords, 0, 0)
    moments = [make_moments(basis_table, vector)]
    for tree_level in range(1, top_level):
        moments.append(upward(moments[-1]))
    local_terms = [coupling_block(jnp.pad(moments[tree_level], ((3, 3), (3, 3), (0, 0), (0, 0))), 0, 0, tree_level) for tree_level in range(top_level)]
    summed = local_terms[top_level - 1]
    for tree_level in range(top_level - 1, 0, -1):
        summed = downward(summed) + local_terms[tree_level - 1]
    return near_part + evaluate_far(basis_table, summed)
```

```python
import functools

import jax
import jax.numpy as jnp
import numpy as np
from jax import lax
from jax.experimental import pallas as pl
from jax.experimental.pallas import tpu as pltpu
from jax.sharding import PartitionSpec as P

QUAD_WEIGHT = 1.0 / 64.0
SMOOTHING = 0.01
CHEB_NODES = np.cos((2.0 * np.arange(4) + 1.0) * np.pi / 8.0)
SIDE = 4
F32 = jnp.float32
BF16 = jnp.bfloat16
MESH = pl.DeviceIdType.MESH
DIRECTIONS = [(-1, 0), (1, 0), (0, -1), (0, 1), (-1, -1), (-1, 1), (1, -1), (1, 1)]


def poly_values(points):
    second = 2.0 * points * points - 1.0
    third = 2.0 * points * second - points
    return (points, second, third)


def cheb_numpy(values):
    nodes_one, nodes_two, nodes_three = poly_values(CHEB_NODES)
    first, second, third = poly_values(values)
    return 0.25 + 0.5 * (
        first[..., None] * nodes_one
        + second[..., None] * nodes_two
        + third[..., None] * nodes_three
    )


def transfer_table():
    halves = [cheb_numpy((CHEB_NODES + 2.0 * side_bit - 1.0) / 2.0) for side_bit in range(2)]
    same_node = np.eye(4)
    blocks = [
        [
            (
                halves[row_bit][:, None, None, :, None, None]
                * halves[col_bit][None, :, None, None, :, None]
                * same_node[None, None, :, None, None, :]
            ).reshape(64, 64)
            for col_bit in range(2)
        ]
        for row_bit in range(2)
    ]
    return np.array(blocks)


def couple_table(tree_level):
    box_width = 2.0**tree_level
    across = 0.5 * box_width * CHEB_NODES
    height = 0.5 + 0.5 * CHEB_NODES
    target = np.stack(np.meshgrid(across, across, height, indexing="ij"), -1).reshape(64, 3)
    table_rows = []
    for row_shift in range(-3, 4):
        table_line = []
        for col_shift in range(-3, 4):
            source = target + np.array([row_shift * box_width, col_shift * box_width, 0.0])
            spacing = target[:, None, :] - source[None, :, :]
            values = QUAD_WEIGHT / np.sqrt(np.sum(spacing * spacing, -1) + SMOOTHING)
            far_flag = float(max(abs(row_shift), abs(col_shift)) >= 2)
            table_line.append(values * far_flag)
        table_rows.append(table_line)
    return np.array(table_rows)


def parent_couplings(tree_level):
    table = couple_table(tree_level).astype(np.float32)
    full = np.zeros((3, 3, 2, 2, 64, 2, 2, 64), np.float32)
    for pi in range(3):
        for pj in range(3):
            for sd in range(2):
                for se in range(2):
                    for td in range(2):
                        for te in range(2):
                            u = 2 * (pi - 1) + sd - td
                            v = 2 * (pj - 1) + se - te
                            full[pi, pj, sd, se, :, td, te, :] = table[u + 3, v + 3].T
    return full.reshape(2304, 256)


def halves_numpy(values):
    values = np.asarray(values, np.float32)
    high = values.astype(BF16)
    low = (values - high.astype(np.float32)).astype(BF16)
    return high, low


def halves(values):
    high = values.astype(BF16).astype(F32)
    return high, values - high


def rows_of_halves(values):
    high, low = halves(values)
    return jnp.concatenate([high, low], 0).astype(BF16)


def mm(left, right):
    return jnp.dot(left, right, preferred_element_type=F32)


def mm_nt(left, right):
    return lax.dot_general(left, right, (((1,), (1,)), ((), ())), preferred_element_type=F32)


def mm_split(values, high, low):
    rows = values.shape[0]
    stacked = rows_of_halves(values)
    first = mm(stacked, high)
    second = mm(stacked[:rows], low)
    return first[:rows] + first[rows:] + second


def wide_node(points, coefs):
    first, second, third = poly_values(points)
    return 0.25 + 0.5 * (first * coefs[0] + second * coefs[1] + third * coefs[2])


def body(
    leaf_total,
    sub_total,
    coarse_levels,
    coords_ref,
    vector_ref,
    node_ref,
    up_ref,
    down_ref,
    fine_hbm,
    coarse_hbm,
    out_ref,
    pack,
    basis,
    flipped,
    near,
    mom,
    gathered,
    level_mom,
    fine_w,
    coarse_w,
    weight_sem,
    coarse_sem,
    pack_send,
    pack_recv,
    mom_send,
    mom_recv,
    all_send,
    all_recv,
):
    leaf_at = lax.axis_index("leaf")
    sub_at = lax.axis_index("sub")
    me = leaf_at * sub_total + sub_at
    count = leaf_total * sub_total

    def peer(step):
        other = lax.rem(me + step, count)
        return other, {"leaf": other // sub_total, "sub": lax.rem(other, sub_total)}

    fine_copy = pltpu.make_async_copy(fine_hbm, fine_w, weight_sem)
    fine_copy.start()
    coarse_copies = []
    for pos in range(coarse_levels):
        row_bit = lax.rem(leaf_at // 2**pos, 2)
        col_bit = lax.rem(sub_at // 2**pos, 2)
        coarse_copies.append(
            pltpu.make_async_copy(
                coarse_hbm.at[pos, 2 * row_bit + col_bit], coarse_w.at[pos], coarse_sem.at[pos]
            )
        )
        coarse_copies[-1].start()

    empty = jnp.zeros((8, 256), F32)
    for k in range(SIDE + 2):
        pack[0, k] = empty
        pack[SIDE + 1, k] = empty
        pack[k, 0] = empty
        pack[k, SIDE + 1] = empty
    for k in range(4):
        mom[0, k] = empty
        mom[3, k] = empty
        mom[k, 0] = empty
        mom[k, 3] = empty

    barrier = pltpu.get_barrier_semaphore()

    def greet(step, carry):
        _, where = peer(step)
        pl.semaphore_signal(barrier, inc=1, device_id=where, device_id_type=MESH)
        return carry

    lax.fori_loop(1, count, greet, 0)

    row_start = (leaf_at * SIDE).astype(F32) + 0.5
    col_start = (sub_at * SIDE).astype(F32) + 0.5
    for i in range(SIDE):
        for j in range(SIDE):
            pack[i + 1, j + 1, 0:1] = coords_ref[0, i, j : j + 1] - (row_start + float(i))
            pack[i + 1, j + 1, 1:2] = coords_ref[1, i, j : j + 1] - (col_start + float(j))
            pack[i + 1, j + 1, 2:3] = coords_ref[2, i, j : j + 1] - 0.5
            pack[i + 1, j + 1, 3:4] = jnp.zeros((1, 256), F32)
            for c in range(4):
                pack[i + 1, j + 1, 4 + c : 5 + c] = vector_ref[c, i, j : j + 1]

    pl.semaphore_wait(barrier, count - 1)

    def edge(inner, shift):
        if shift == 0:
            return pl.ds(1, inner), pl.ds(1, inner)
        if shift < 0:
            return pl.ds(1, 1), pl.ds(inner + 1, 1)
        return pl.ds(inner, 1), pl.ds(0, 1)

    def halo(ref, inner, send, recv):
        copies = []
        for k, (di, dj) in enumerate(DIRECTIONS):
            src_i, dst_i = edge(inner, di)
            src_j, dst_j = edge(inner, dj)
            to_ok = (leaf_at + di >= 0) & (leaf_at + di < leaf_total)
            to_ok = to_ok & (sub_at + dj >= 0) & (sub_at + dj < sub_total)
            from_ok = (leaf_at - di >= 0) & (leaf_at - di < leaf_total)
            from_ok = from_ok & (sub_at - dj >= 0) & (sub_at - dj < sub_total)
            copy = pltpu.make_async_remote_copy(
                src_ref=ref.at[src_i, src_j],
                dst_ref=ref.at[dst_i, dst_j],
                send_sem=send.at[k],
                recv_sem=recv.at[k],
                device_id={"leaf": leaf_at + di, "sub": sub_at + dj},
                device_id_type=MESH,
            )
            copies.append((copy, to_ok, from_ok))
        for copy, to_ok, _ in copies:
            pl.when(to_ok)(copy.start)
        return copies

    def halo_wait(copies):
        for copy, to_ok, from_ok in copies:
            pl.when(to_ok)(copy.wait_send)
            pl.when(from_ok)(copy.wait_recv)

    pack_copies = halo(pack, SIDE, pack_send, pack_recv)

    nodes = np.array(poly_values(CHEB_NODES))
    y_coefs = [node_ref[n] for n in range(3)]
    z_coefs = [node_ref[3 + n] for n in range(3)]
    row_id = lax.broadcasted_iota(jnp.int32, (8, 256), 0)
    for i in range(SIDE):
        for j in range(SIDE):
            box = pack[i + 1, j + 1]
            y_part = wide_node(2.0 * box[1:2], y_coefs)
            z_part = wide_node(2.0 * box[2:3], z_coefs)
            yz_part = y_part * z_part
            x_first = poly_values(2.0 * box[0:1])
            planes = []
            for k in range(4):
                weight = 0.25 + 0.5 * sum(x_first[n] * float(nodes[n, k]) for n in range(3))
                planes.append(yz_part * weight)
            wide = rows_of_halves(jnp.concatenate(planes, 0))
            basis[i * SIDE + j] = wide
            vec = box[4:8]
            v_high, v_low = halves(vec)
            both = jnp.concatenate([v_high, v_low, jnp.zeros((8, 256), F32)], 0).astype(BF16)
            got = mm_nt(both, wide)
            piece = got[0:4, 0:64] + got[4:8, 0:64] + got[0:4, 64:128]
            at = 64 * (2 * (i % 2) + j % 2)
            mom[1 + i // 2, 1 + j // 2, 0:4, at : at + 64] = piece
            mom[1 + i // 2, 1 + j // 2, 4:8, at : at + 64] = jnp.zeros((4, 64), F32)
    mom_copies = halo(mom, 2, mom_send, mom_recv)
    parents = jnp.concatenate([mom[1, 1], mom[1, 2], mom[2, 1], mom[2, 2]], 0)
    raised = mm_split(parents, up_ref[0], up_ref[1])
    gathered[me] = jnp.concatenate([raised[8 * k : 8 * k + 8] for k in range(4)], 1)

    def spread_copy(step, own_slot):
        other, where = peer(step)
        slot = me if own_slot else other
        return pltpu.make_async_remote_copy(
            src_ref=gathered.at[me],
            dst_ref=gathered.at[slot],
            send_sem=all_send.at[other],
            recv_sem=all_recv.at[slot],
            device_id=where,
            device_id_type=MESH,
        )

    def spread(step, carry):
        spread_copy(step, True).start()
        return carry

    lax.fori_loop(1, count, spread, 0)

    ones = jnp.ones((8, 256), F32)

    def parts_of(tile):
        first = tile.astype(BF16).astype(F32)
        rest = tile - first
        second = rest.astype(BF16).astype(F32)
        return first, second, rest - second

    def squares(tile):
        sq = tile * tile
        return sq[0:1] + sq[1:2] + sq[2:3]

    for i in range(SIDE):
        for j in range(SIDE):
            box = pack[i + 1, j + 1]
            first, second, third = parts_of(jnp.where(row_id < 3, box, 0.0))
            n_first, n_second, n_third = parts_of(squares(box))
            groups = []
            for piece, norm in (
                (first, n_first),
                (first, n_second),
                (first, n_third),
            ):
                tile = jnp.where(row_id == 3, ones, -2.0 * piece)
                groups.append(jnp.where(row_id == 4, norm, tile))
            groups += [-2.0 * second, -2.0 * second, -2.0 * third]
            groups.append(jnp.zeros((80, 256), F32))
            flipped[i * SIDE + j] = jnp.concatenate(groups, 0).T.astype(BF16)

    halo_wait(pack_copies)

    def near_box(box_at, carry):
        i = box_at // SIDE
        j = lax.rem(box_at, SIDE)
        target = flipped[box_at][:, :48]
        total = jnp.zeros((256, 16), F32)
        for di in range(3):
            for dj in range(3):
                box = pack[i + di, j + dj]
                moved = jnp.where(row_id == 0, box + float(di - 1), box)
                moved = jnp.where(row_id == 1, box + float(dj - 1), moved)
                norm = squares(moved) + SMOOTHING
                tile = jnp.where(row_id == 3, norm, jnp.where(row_id < 3, moved, 0.0))
                first, second, third = parts_of(tile)
                stacked = [
                    jnp.where(row_id == 4, ones, first),
                    jnp.where(row_id == 4, ones, second),
                    jnp.where(row_id == 4, ones, third),
                    first,
                    second,
                    first,
                ]
                source = jnp.concatenate(stacked, 0).astype(BF16)
                v_high, v_low = halves(box[4:8])
                vec = jnp.concatenate([v_high, v_low, jnp.zeros((8, 256), F32)], 0).astype(BF16)
                kern = lax.rsqrt(mm(target, source))
                high = kern.astype(BF16)
                low = (kern - high.astype(F32)).astype(BF16)
                total = total + mm_nt(high, vec) + mm_nt(low, vec)
        wide = jnp.concatenate([total, jnp.zeros((256, 112), F32)], 1).T
        near[box_at] = QUAD_WEIGHT * (wide[0:4] + wide[4:8])
        return carry

    lax.fori_loop(0, SIDE * SIDE, near_box, 0)

    def spread_wait(step, carry):
        spread_copy(step, True).wait_send()
        spread_copy(step, False).wait_recv()
        return carry

    lax.fori_loop(1, count, spread_wait, 0)

    def padded_read(row, col):
        row_ok = (row >= 0) & (row < leaf_total)
        col_ok = (col >= 0) & (col < sub_total)
        at = jnp.clip(row, 0, leaf_total - 1) * sub_total + jnp.clip(col, 0, sub_total - 1)
        return jnp.where(row_ok & col_ok, gathered[at], 0.0)

    for copy in coarse_copies:
        copy.wait()
    current = gathered[...].reshape(count * 8, 256)
    rows_here, cols_here = leaf_total, sub_total
    coarse_local = []
    for pos in range(coarse_levels):
        raised = mm_split(current, up_ref[0], up_ref[1])
        p_rows, p_cols = rows_here // 2, cols_here // 2
        for a in range(p_rows + 2):
            for b in range(p_cols + 2):
                if a in (0, p_rows + 1) or b in (0, p_cols + 1):
                    level_mom[pos, a, b] = empty
        tiles = []
        for a in range(p_rows):
            for b in range(p_cols):
                kids = []
                for d in range(2):
                    for e in range(2):
                        at = 8 * ((2 * a + d) * cols_here + 2 * b + e)
                        kids.append(raised[at : at + 8])
                tile = jnp.concatenate(kids, 1)
                level_mom[pos, a + 1, b + 1] = tile
                tiles.append(tile)
        pi = leaf_at // 2 ** (pos + 1)
        pj = sub_at // 2 ** (pos + 1)
        window = jnp.concatenate(
            [level_mom[pos, pi + a, pj + b] for a in range(3) for b in range(3)], 1
        )
        got = mm(rows_of_halves(window), coarse_w[pos])
        coarse_local.append(got[0:8, 0:64] + got[8:16, 0:64] + got[0:8, 64:128])
        current = jnp.concatenate(tiles, 0)
        rows_here, cols_here = p_rows, p_cols

    summed = coarse_local[-1]
    for pos in range(coarse_levels - 1, 0, -1):
        children = mm_split(summed, down_ref[0], down_ref[1])
        row_bit = lax.rem(leaf_at // 2 ** (pos - 1), 2)
        col_bit = lax.rem(sub_at // 2 ** (pos - 1), 2)
        child = 2 * row_bit + col_bit
        summed = coarse_local[pos - 1]
        for k in range(4):
            summed = summed + jnp.where(child == k, children[:, 64 * k : 64 * k + 64], 0.0)

    halo_wait(mom_copies)
    fine_copy.wait()
    window = jnp.concatenate(
        [padded_read(leaf_at + a, sub_at + b) for a in (-1, 0, 1) for b in (-1, 0, 1)], 1
    )
    level_one = mm_split(summed, down_ref[0], down_ref[1]) + mm_split(
        window, fine_w[1, 0], fine_w[1, 1]
    )
    stacked = jnp.concatenate([level_one[:, 64 * k : 64 * k + 64] for k in range(4)], 0)
    window = jnp.concatenate(
        [
            jnp.concatenate([mom[a + di, b + dj] for a in range(2) for b in range(2)], 0)
            for di in range(3)
            for dj in range(3)
        ],
        1,
    )
    level_zero = mm_split(stacked, down_ref[0], down_ref[1]) + mm_split(
        window, fine_w[0, 0], fine_w[0, 1]
    )
    for i in range(SIDE):
        for j in range(SIDE):
            row = 8 * (2 * (i // 2) + j // 2)
            at = 64 * (2 * (i % 2) + j % 2)
            coef = level_zero[row : row + 8, at : at + 64]
            high, low = halves(coef)
            wide = basis[i * SIDE + j]
            left = jnp.concatenate([high, low], 0).astype(BF16)
            got = mm(left, wide[:64])
            got_low = mm(left, wide[64:])
            result = near[i * SIDE + j] + got[0:4] + got[8:12] + got_low[0:4]
            for c in range(4):
                out_ref[c, i, j : j + 1] = result[c : c + 1]


def local(coords, vector):
    leaf_total = lax.axis_size("leaf")
    sub_total = lax.axis_size("sub")
    count = leaf_total * sub_total
    top_level = (SIDE * sub_total).bit_length() - 1
    coarse_levels = top_level - 2

    nodes = np.array(poly_values(CHEB_NODES))
    index = np.arange(16)
    node_table = np.concatenate([nodes[:, index // 4], nodes[:, index % 4]], 0)
    node_table = np.repeat(node_table[:, :, None], 256, 2).astype(np.float32)
    table = transfer_table()
    up = np.stack(halves_numpy(table.reshape(256, 64)))
    down = np.stack(halves_numpy(table.reshape(256, 64).T))
    fine = np.stack([np.stack(halves_numpy(parent_couplings(level))) for level in range(2)])
    coarse = []
    for level in range(2, top_level):
        high, low = halves_numpy(parent_couplings(level))
        high = high.reshape(2304, 4, 64).transpose(1, 0, 2)
        low = low.reshape(2304, 4, 64).transpose(1, 0, 2)
        coarse.append(np.concatenate([high, low], 2))
    coarse = np.stack(coarse)

    vmem = pl.BlockSpec(memory_space=pltpu.VMEM)
    hbm = pl.BlockSpec(memory_space=pl.ANY)
    dma = pltpu.SemaphoreType.DMA
    return pl.pallas_call(
        functools.partial(body, leaf_total, sub_total, coarse_levels),
        out_shape=jax.ShapeDtypeStruct(vector.shape, F32),
        in_specs=[vmem, vmem, vmem, vmem, vmem, hbm, hbm],
        out_specs=vmem,
        scratch_shapes=[
            pltpu.VMEM((SIDE + 2, SIDE + 2, 8, 256), F32),
            pltpu.VMEM((SIDE * SIDE, 128, 256), BF16),
            pltpu.VMEM((SIDE * SIDE, 256, 128), BF16),
            pltpu.VMEM((SIDE * SIDE, 4, 256), F32),
            pltpu.VMEM((4, 4, 8, 256), F32),
            pltpu.VMEM((count, 8, 256), F32),
            pltpu.VMEM((coarse_levels, leaf_total // 2 + 2, sub_total // 2 + 2, 8, 256), F32),
            pltpu.VMEM((2, 2, 2304, 256), BF16),
            pltpu.VMEM((coarse_levels, 2304, 128), BF16),
            dma,
            dma((coarse_levels,)),
            dma((8,)),
            dma((8,)),
            dma((8,)),
            dma((8,)),
            dma((count,)),
            dma((count,)),
        ],
        compiler_params=pltpu.CompilerParams(
            collective_id=0, has_side_effects=True, vmem_limit_bytes=40 * 1024 * 1024
        ),
    )(coords, vector, node_table, up, down, fine, coarse)


def solution(mesh):
    placed = (P(None, ("groups", "leaf"), "sub", None), P("rep", ("groups", "leaf"), "sub", None))
    return jax.shard_map(
        local,
        mesh=mesh,
        in_specs=placed,
        out_specs=P("rep", ("groups", "leaf"), "sub", None),
        check_vma=False,
    )
```

```python
import functools

import jax
import jax.numpy as jnp
import numpy as np
from jax import lax
from jax.experimental import pallas as pl
from jax.experimental.pallas import tpu as pltpu
from jax.sharding import PartitionSpec as P

QUAD_WEIGHT = 1.0 / 64.0
SMOOTHING = 0.01
CHEB_NODES = np.cos((2.0 * np.arange(4) + 1.0) * np.pi / 8.0)
SIDE = 4
F32 = jnp.float32
BF16 = jnp.bfloat16
MESH = pl.DeviceIdType.MESH
DIRECTIONS = [(-1, 0), (1, 0), (0, -1), (0, 1), (-1, -1), (-1, 1), (1, -1), (1, 1)]


def poly_values(points):
    second = 2.0 * points * points - 1.0
    third = 2.0 * points * second - points
    return (points, second, third)


def cheb_numpy(values):
    nodes_one, nodes_two, nodes_three = poly_values(CHEB_NODES)
    first, second, third = poly_values(values)
    return 0.25 + 0.5 * (
        first[..., None] * nodes_one
        + second[..., None] * nodes_two
        + third[..., None] * nodes_three
    )


def transfer_table():
    halves = [cheb_numpy((CHEB_NODES + 2.0 * side_bit - 1.0) / 2.0) for side_bit in range(2)]
    same_node = np.eye(4)
    blocks = [
        [
            (
                halves[row_bit][:, None, None, :, None, None]
                * halves[col_bit][None, :, None, None, :, None]
                * same_node[None, None, :, None, None, :]
            ).reshape(64, 64)
            for col_bit in range(2)
        ]
        for row_bit in range(2)
    ]
    return np.array(blocks)


def couple_table(tree_level):
    box_width = 2.0**tree_level
    across = 0.5 * box_width * CHEB_NODES
    height = 0.5 + 0.5 * CHEB_NODES
    target = np.stack(np.meshgrid(across, across, height, indexing="ij"), -1).reshape(64, 3)
    table_rows = []
    for row_shift in range(-3, 4):
        table_line = []
        for col_shift in range(-3, 4):
            source = target + np.array([row_shift * box_width, col_shift * box_width, 0.0])
            spacing = target[:, None, :] - source[None, :, :]
            values = QUAD_WEIGHT / np.sqrt(np.sum(spacing * spacing, -1) + SMOOTHING)
            far_flag = float(max(abs(row_shift), abs(col_shift)) >= 2)
            table_line.append(values * far_flag)
        table_rows.append(table_line)
    return np.array(table_rows)


def parent_couplings(tree_level):
    table = couple_table(tree_level).astype(np.float32)
    full = np.zeros((3, 3, 2, 2, 64, 2, 2, 64), np.float32)
    for pi in range(3):
        for pj in range(3):
            for sd in range(2):
                for se in range(2):
                    for td in range(2):
                        for te in range(2):
                            u = 2 * (pi - 1) + sd - td
                            v = 2 * (pj - 1) + se - te
                            full[pi, pj, sd, se, :, td, te, :] = table[u + 3, v + 3].T
    return full.reshape(2304, 256)


def halves_numpy(values):
    values = np.asarray(values, np.float32)
    high = values.astype(BF16)
    low = (values - high.astype(np.float32)).astype(BF16)
    return high, low


def halves(values):
    high = values.astype(BF16).astype(F32)
    return high, values - high


def rows_of_halves(values):
    high, low = halves(values)
    return jnp.concatenate([high, low], 0).astype(BF16)


def mm(left, right):
    return jnp.dot(left, right, preferred_element_type=F32)


def mm_nt(left, right):
    return lax.dot_general(left, right, (((1,), (1,)), ((), ())), preferred_element_type=F32)


def mm_split(values, high, low):
    rows = values.shape[0]
    stacked = rows_of_halves(values)
    first = mm(stacked, high)
    second = mm(stacked[:rows], low)
    return first[:rows] + first[rows:] + second


def wide_node(points, coefs):
    first, second, third = poly_values(points)
    return 0.25 + 0.5 * (first * coefs[0] + second * coefs[1] + third * coefs[2])


def body(
    leaf_total,
    sub_total,
    coarse_levels,
    coords_hbm,
    vector_hbm,
    node_hbm,
    up_hbm,
    down_hbm,
    fine_hbm,
    coarse_hbm,
    out_ref,
    coords_ref,
    vector_ref,
    node_ref,
    up_ref,
    down_ref,
    pack,
    basis,
    flipped,
    near,
    mom,
    gathered,
    level_mom,
    fine_w,
    coarse_w,
    input_sem,
    weight_sem,
    coarse_sem,
    pack_send,
    pack_recv,
    mom_send,
    mom_recv,
    all_send,
    all_recv,
):
    leaf_at = lax.axis_index("leaf")
    sub_at = lax.axis_index("sub")
    me = leaf_at * sub_total + sub_at
    count = leaf_total * sub_total

    def peer(step):
        other = lax.rem(me + step, count)
        return other, {"leaf": other // sub_total, "sub": lax.rem(other, sub_total)}

    input_copies = [
        pltpu.make_async_copy(src, dst, input_sem.at[k])
        for k, (src, dst) in enumerate(
            (
                (coords_hbm, coords_ref),
                (vector_hbm, vector_ref),
                (node_hbm, node_ref),
                (up_hbm, up_ref),
                (down_hbm, down_ref),
            )
        )
    ]
    for copy in input_copies:
        copy.start()
    fine_copy = pltpu.make_async_copy(fine_hbm, fine_w, weight_sem)
    fine_copy.start()
    coarse_copies = []
    for pos in range(coarse_levels):
        row_bit = lax.rem(leaf_at // 2**pos, 2)
        col_bit = lax.rem(sub_at // 2**pos, 2)
        coarse_copies.append(
            pltpu.make_async_copy(
                coarse_hbm.at[pos, 2 * row_bit + col_bit], coarse_w.at[pos], coarse_sem.at[pos]
            )
        )
        coarse_copies[-1].start()

    empty = jnp.zeros((8, 256), F32)
    for k in range(SIDE + 2):
        pack[0, k] = empty
        pack[SIDE + 1, k] = empty
        pack[k, 0] = empty
        pack[k, SIDE + 1] = empty
    for k in range(4):
        mom[0, k] = empty
        mom[3, k] = empty
        mom[k, 0] = empty
        mom[k, 3] = empty

    barrier = pltpu.get_barrier_semaphore()

    def greet(step, carry):
        _, where = peer(step)
        pl.semaphore_signal(barrier, inc=1, device_id=where, device_id_type=MESH)
        return carry

    lax.fori_loop(1, count, greet, 0)

    input_copies[0].wait()
    input_copies[1].wait()
    row_start = (leaf_at * SIDE).astype(F32) + 0.5
    col_start = (sub_at * SIDE).astype(F32) + 0.5
    for i in range(SIDE):
        for j in range(SIDE):
            pack[i + 1, j + 1, 0:1] = coords_ref[0, i, j : j + 1] - (row_start + float(i))
            pack[i + 1, j + 1, 1:2] = coords_ref[1, i, j : j + 1] - (col_start + float(j))
            pack[i + 1, j + 1, 2:3] = coords_ref[2, i, j : j + 1] - 0.5
            pack[i + 1, j + 1, 3:4] = jnp.zeros((1, 256), F32)
            for c in range(4):
                pack[i + 1, j + 1, 4 + c : 5 + c] = vector_ref[c, i, j : j + 1]

    pl.semaphore_wait(barrier, count - 1)

    def edge(inner, shift):
        if shift == 0:
            return pl.ds(1, inner), pl.ds(1, inner)
        if shift < 0:
            return pl.ds(1, 1), pl.ds(inner + 1, 1)
        return pl.ds(inner, 1), pl.ds(0, 1)

    def halo(ref, inner, send, recv):
        copies = []
        for k, (di, dj) in enumerate(DIRECTIONS):
            src_i, dst_i = edge(inner, di)
            src_j, dst_j = edge(inner, dj)
            to_ok = (leaf_at + di >= 0) & (leaf_at + di < leaf_total)
            to_ok = to_ok & (sub_at + dj >= 0) & (sub_at + dj < sub_total)
            from_ok = (leaf_at - di >= 0) & (leaf_at - di < leaf_total)
            from_ok = from_ok & (sub_at - dj >= 0) & (sub_at - dj < sub_total)
            copy = pltpu.make_async_remote_copy(
                src_ref=ref.at[src_i, src_j],
                dst_ref=ref.at[dst_i, dst_j],
                send_sem=send.at[k],
                recv_sem=recv.at[k],
                device_id={"leaf": leaf_at + di, "sub": sub_at + dj},
                device_id_type=MESH,
            )
            copies.append((copy, to_ok, from_ok))
        for copy, to_ok, _ in copies:
            pl.when(to_ok)(copy.start)
        return copies

    def halo_wait(copies):
        for copy, to_ok, from_ok in copies:
            pl.when(to_ok)(copy.wait_send)
            pl.when(from_ok)(copy.wait_recv)

    pack_copies = halo(pack, SIDE, pack_send, pack_recv)

    nodes = np.array(poly_values(CHEB_NODES))
    for copy in input_copies[2:]:
        copy.wait()
    y_coefs = [node_ref[n] for n in range(3)]
    z_coefs = [node_ref[3 + n] for n in range(3)]
    row_id = lax.broadcasted_iota(jnp.int32, (8, 256), 0)
    for i in range(SIDE):
        for j in range(SIDE):
            box = pack[i + 1, j + 1]
            y_part = wide_node(2.0 * box[1:2], y_coefs)
            z_part = wide_node(2.0 * box[2:3], z_coefs)
            yz_part = y_part * z_part
            x_first = poly_values(2.0 * box[0:1])
            planes = []
            for k in range(4):
                weight = 0.25 + 0.5 * sum(x_first[n] * float(nodes[n, k]) for n in range(3))
                planes.append(yz_part * weight)
            wide = rows_of_halves(jnp.concatenate(planes, 0))
            basis[i * SIDE + j] = wide
            vec = box[4:8]
            v_high, v_low = halves(vec)
            both = jnp.concatenate([v_high, v_low, jnp.zeros((8, 256), F32)], 0).astype(BF16)
            got = mm_nt(both, wide)
            piece = got[0:4, 0:64] + got[4:8, 0:64] + got[0:4, 64:128]
            at = 64 * (2 * (i % 2) + j % 2)
            mom[1 + i // 2, 1 + j // 2, 0:4, at : at + 64] = piece
            mom[1 + i // 2, 1 + j // 2, 4:8, at : at + 64] = jnp.zeros((4, 64), F32)
    mom_copies = halo(mom, 2, mom_send, mom_recv)
    parents = jnp.concatenate([mom[1, 1], mom[1, 2], mom[2, 1], mom[2, 2]], 0)
    raised = mm_split(parents, up_ref[0], up_ref[1])
    gathered[me] = jnp.concatenate([raised[8 * k : 8 * k + 8] for k in range(4)], 1)

    def spread_copy(step, own_slot):
        other, where = peer(step)
        slot = me if own_slot else other
        return pltpu.make_async_remote_copy(
            src_ref=gathered.at[me],
            dst_ref=gathered.at[slot],
            send_sem=all_send.at[other],
            recv_sem=all_recv.at[slot],
            device_id=where,
            device_id_type=MESH,
        )

    def spread(step, carry):
        spread_copy(step, True).start()
        return carry

    lax.fori_loop(1, count, spread, 0)

    ones = jnp.ones((8, 256), F32)

    def parts_of(tile):
        first = tile.astype(BF16).astype(F32)
        rest = tile - first
        second = rest.astype(BF16).astype(F32)
        return first, second, rest - second

    def squares(tile):
        sq = tile * tile
        return sq[0:1] + sq[1:2] + sq[2:3]

    def flip(i, j):
        box = pack[i, j]
        first, second, third = parts_of(jnp.where(row_id < 3, box, 0.0))
        n_first, n_second, n_third = parts_of(squares(box))
        groups = []
        for norm in (n_first, n_second, n_third):
            tile = jnp.where(row_id == 3, ones, -2.0 * first)
            groups.append(jnp.where(row_id == 4, norm, tile))
        groups += [-2.0 * second, -2.0 * second, -2.0 * third]
        groups.append(jnp.zeros((80, 256), F32))
        flipped[i * (SIDE + 2) + j] = jnp.concatenate(groups, 0).T.astype(BF16)

    for i in range(SIDE):
        for j in range(SIDE):
            flip(i + 1, j + 1)
    halo_wait(pack_copies)
    for k in range(SIDE + 2):
        flip(0, k)
        flip(SIDE + 1, k)
    for k in range(SIDE):
        flip(k + 1, 0)
        flip(k + 1, SIDE + 1)

    def near_box(box_at, carry):
        i = box_at // SIDE
        j = lax.rem(box_at, SIDE)
        target = pack[i + 1, j + 1]
        total = jnp.zeros((16, 256), F32)
        for di in range(3):
            for dj in range(3):
                moved = jnp.where(row_id == 0, target + float(1 - di), target)
                moved = jnp.where(row_id == 1, target + float(1 - dj), moved)
                norm = squares(moved) + SMOOTHING
                tile = jnp.where(row_id == 3, norm, jnp.where(row_id < 3, moved, 0.0))
                first, second, third = parts_of(tile)
                stacked = [
                    jnp.where(row_id == 4, ones, first),
                    jnp.where(row_id == 4, ones, second),
                    jnp.where(row_id == 4, ones, third),
                    first,
                    second,
                    first,
                ]
                feature = jnp.concatenate(stacked, 0).astype(BF16)
                v_high, v_low = halves(pack[i + di, j + dj, 4:8])
                vec = jnp.concatenate([v_high, v_low, jnp.zeros((8, 256), F32)], 0).astype(BF16)
                source = (i + di) * (SIDE + 2) + j + dj
                for half in range(2):
                    part = slice(128 * half, 128 * half + 128)
                    kern = lax.rsqrt(mm(flipped[source, part, :48], feature))
                    high = kern.astype(BF16)
                    low = (kern - high.astype(F32)).astype(BF16)
                    weights = jnp.concatenate([high, low], 0)
                    total = total + mm(jnp.concatenate([vec[:, part]] * 2, 1), weights)
        near[box_at] = QUAD_WEIGHT * (total[0:4] + total[4:8])
        return carry

    lax.fori_loop(0, SIDE * SIDE, near_box, 0)

    def spread_wait(step, carry):
        spread_copy(step, True).wait_send()
        spread_copy(step, False).wait_recv()
        return carry

    lax.fori_loop(1, count, spread_wait, 0)

    def padded_read(row, col):
        row_ok = (row >= 0) & (row < leaf_total)
        col_ok = (col >= 0) & (col < sub_total)
        at = jnp.clip(row, 0, leaf_total - 1) * sub_total + jnp.clip(col, 0, sub_total - 1)
        return jnp.where(row_ok & col_ok, gathered[at], 0.0)

    for copy in coarse_copies:
        copy.wait()
    current = gathered[...].reshape(count * 8, 256)
    rows_here, cols_here = leaf_total, sub_total
    coarse_local = []
    for pos in range(coarse_levels):
        raised = mm_split(current, up_ref[0], up_ref[1])
        p_rows, p_cols = rows_here // 2, cols_here // 2
        for a in range(p_rows + 2):
            for b in range(p_cols + 2):
                if a in (0, p_rows + 1) or b in (0, p_cols + 1):
                    level_mom[pos, a, b] = empty
        tiles = []
        for a in range(p_rows):
            for b in range(p_cols):
                kids = []
                for d in range(2):
                    for e in range(2):
                        at = 8 * ((2 * a + d) * cols_here + 2 * b + e)
                        kids.append(raised[at : at + 8])
                tile = jnp.concatenate(kids, 1)
                level_mom[pos, a + 1, b + 1] = tile
                tiles.append(tile)
        pi = leaf_at // 2 ** (pos + 1)
        pj = sub_at // 2 ** (pos + 1)
        window = jnp.concatenate(
            [level_mom[pos, pi + a, pj + b] for a in range(3) for b in range(3)], 1
        )
        got = mm(rows_of_halves(window), coarse_w[pos])
        coarse_local.append(got[0:8, 0:64] + got[8:16, 0:64] + got[0:8, 64:128])
        current = jnp.concatenate(tiles, 0)
        rows_here, cols_here = p_rows, p_cols

    summed = coarse_local[-1]
    for pos in range(coarse_levels - 1, 0, -1):
        children = mm_split(summed, down_ref[0], down_ref[1])
        row_bit = lax.rem(leaf_at // 2 ** (pos - 1), 2)
        col_bit = lax.rem(sub_at // 2 ** (pos - 1), 2)
        child = 2 * row_bit + col_bit
        summed = coarse_local[pos - 1]
        for k in range(4):
            summed = summed + jnp.where(child == k, children[:, 64 * k : 64 * k + 64], 0.0)

    halo_wait(mom_copies)
    fine_copy.wait()
    window = jnp.concatenate(
        [padded_read(leaf_at + a, sub_at + b) for a in (-1, 0, 1) for b in (-1, 0, 1)], 1
    )
    level_one = mm_split(summed, down_ref[0], down_ref[1]) + mm_split(
        window, fine_w[1, 0], fine_w[1, 1]
    )
    stacked = jnp.concatenate([level_one[:, 64 * k : 64 * k + 64] for k in range(4)], 0)
    window = jnp.concatenate(
        [
            jnp.concatenate([mom[a + di, b + dj] for a in range(2) for b in range(2)], 0)
            for di in range(3)
            for dj in range(3)
        ],
        1,
    )
    level_zero = mm_split(stacked, down_ref[0], down_ref[1]) + mm_split(
        window, fine_w[0, 0], fine_w[0, 1]
    )
    for i in range(SIDE):
        for j in range(SIDE):
            row = 8 * (2 * (i // 2) + j // 2)
            at = 64 * (2 * (i % 2) + j % 2)
            coef = level_zero[row : row + 8, at : at + 64]
            high, low = halves(coef)
            wide = basis[i * SIDE + j]
            left = jnp.concatenate([high, low], 0).astype(BF16)
            got = mm(left, wide[:64])
            got_low = mm(left, wide[64:])
            result = near[i * SIDE + j] + got[0:4] + got[8:12] + got_low[0:4]
            for c in range(4):
                out_ref[c, i, j : j + 1] = result[c : c + 1]


def local(coords, vector):
    leaf_total = lax.axis_size("leaf")
    sub_total = lax.axis_size("sub")
    count = leaf_total * sub_total
    top_level = (SIDE * sub_total).bit_length() - 1
    coarse_levels = top_level - 2

    nodes = np.array(poly_values(CHEB_NODES))
    index = np.arange(16)
    node_table = np.concatenate([nodes[:, index // 4], nodes[:, index % 4]], 0)
    node_table = np.repeat(node_table[:, :, None], 256, 2).astype(np.float32)
    table = transfer_table()
    up = np.stack(halves_numpy(table.reshape(256, 64)))
    down = np.stack(halves_numpy(table.reshape(256, 64).T))
    fine = np.stack([np.stack(halves_numpy(parent_couplings(level))) for level in range(2)])
    coarse = []
    for level in range(2, top_level):
        high, low = halves_numpy(parent_couplings(level))
        high = high.reshape(2304, 4, 64).transpose(1, 0, 2)
        low = low.reshape(2304, 4, 64).transpose(1, 0, 2)
        coarse.append(np.concatenate([high, low], 2))
    coarse = np.stack(coarse)

    vmem = pl.BlockSpec(memory_space=pltpu.VMEM)
    hbm = pl.BlockSpec(memory_space=pltpu.HBM)
    dma = pltpu.SemaphoreType.DMA
    return pl.pallas_call(
        functools.partial(body, leaf_total, sub_total, coarse_levels),
        out_shape=jax.ShapeDtypeStruct(vector.shape, F32),
        in_specs=[hbm] * 7,
        out_specs=vmem,
        scratch_shapes=[
            pltpu.VMEM(coords.shape, F32),
            pltpu.VMEM(vector.shape, F32),
            pltpu.VMEM(node_table.shape, F32),
            pltpu.VMEM(up.shape, BF16),
            pltpu.VMEM(down.shape, BF16),
            pltpu.VMEM((SIDE + 2, SIDE + 2, 8, 256), F32),
            pltpu.VMEM((SIDE * SIDE, 128, 256), BF16),
            pltpu.VMEM(((SIDE + 2) ** 2, 256, 128), BF16),
            pltpu.VMEM((SIDE * SIDE, 4, 256), F32),
            pltpu.VMEM((4, 4, 8, 256), F32),
            pltpu.VMEM((count, 8, 256), F32),
            pltpu.VMEM((coarse_levels, leaf_total // 2 + 2, sub_total // 2 + 2, 8, 256), F32),
            pltpu.VMEM((2, 2, 2304, 256), BF16),
            pltpu.VMEM((coarse_levels, 2304, 128), BF16),
            dma((5,)),
            dma,
            dma((coarse_levels,)),
            dma((8,)),
            dma((8,)),
            dma((8,)),
            dma((8,)),
            dma((count,)),
            dma((count,)),
        ],
        compiler_params=pltpu.CompilerParams(
            collective_id=0, has_side_effects=True, vmem_limit_bytes=40 * 1024 * 1024
        ),
    )(coords, vector, node_table, up, down, fine, coarse)


def solution(mesh):
    placed = (P(None, ("groups", "leaf"), "sub", None), P("rep", ("groups", "leaf"), "sub", None))
    return jax.shard_map(
        local,
        mesh=mesh,
        in_specs=placed,
        out_specs=P("rep", ("groups", "leaf"), "sub", None),
        check_vma=False,
    )
```

```python
import functools

import jax
import jax.numpy as jnp
import numpy as np
from jax import lax
from jax.experimental import pallas as pl
from jax.experimental.pallas import tpu as pltpu
from jax.sharding import PartitionSpec as P

QUAD_WEIGHT = 1.0 / 64.0
SMOOTHING = 0.01
CHEB_NODES = np.cos((2.0 * np.arange(4) + 1.0) * np.pi / 8.0)
SIDE = 4
F32 = jnp.float32
BF16 = jnp.bfloat16
MESH = pl.DeviceIdType.MESH
DIRECTIONS = [(-1, 0), (1, 0), (0, -1), (0, 1), (-1, -1), (-1, 1), (1, -1), (1, 1)]


def poly_values(points):
    second = 2.0 * points * points - 1.0
    third = 2.0 * points * second - points
    return (points, second, third)


def cheb_numpy(values):
    nodes_one, nodes_two, nodes_three = poly_values(CHEB_NODES)
    first, second, third = poly_values(values)
    return 0.25 + 0.5 * (
        first[..., None] * nodes_one
        + second[..., None] * nodes_two
        + third[..., None] * nodes_three
    )


def transfer_table():
    halves = [cheb_numpy((CHEB_NODES + 2.0 * side_bit - 1.0) / 2.0) for side_bit in range(2)]
    same_node = np.eye(4)
    blocks = [
        [
            (
                halves[row_bit][:, None, None, :, None, None]
                * halves[col_bit][None, :, None, None, :, None]
                * same_node[None, None, :, None, None, :]
            ).reshape(64, 64)
            for col_bit in range(2)
        ]
        for row_bit in range(2)
    ]
    return np.array(blocks)


def couple_table(tree_level):
    box_width = 2.0**tree_level
    across = 0.5 * box_width * CHEB_NODES
    height = 0.5 + 0.5 * CHEB_NODES
    target = np.stack(np.meshgrid(across, across, height, indexing="ij"), -1).reshape(64, 3)
    table_rows = []
    for row_shift in range(-3, 4):
        table_line = []
        for col_shift in range(-3, 4):
            source = target + np.array([row_shift * box_width, col_shift * box_width, 0.0])
            spacing = target[:, None, :] - source[None, :, :]
            values = QUAD_WEIGHT / np.sqrt(np.sum(spacing * spacing, -1) + SMOOTHING)
            far_flag = float(max(abs(row_shift), abs(col_shift)) >= 2)
            table_line.append(values * far_flag)
        table_rows.append(table_line)
    return np.array(table_rows)


def parent_couplings(tree_level):
    table = couple_table(tree_level).astype(np.float32)
    full = np.zeros((3, 3, 2, 2, 64, 2, 2, 64), np.float32)
    for pi in range(3):
        for pj in range(3):
            for sd in range(2):
                for se in range(2):
                    for td in range(2):
                        for te in range(2):
                            u = 2 * (pi - 1) + sd - td
                            v = 2 * (pj - 1) + se - te
                            full[pi, pj, sd, se, :, td, te, :] = table[u + 3, v + 3].T
    return full.reshape(2304, 256)


def halves_numpy(values):
    values = np.asarray(values, np.float32)
    high = values.astype(BF16)
    low = (values - high.astype(np.float32)).astype(BF16)
    return high, low


def halves(values):
    high = values.astype(BF16).astype(F32)
    return high, values - high


def rows_of_halves(values):
    high, low = halves(values)
    return jnp.concatenate([high, low], 0).astype(BF16)


def mm(left, right):
    return jnp.dot(left, right, preferred_element_type=F32)


def mm_nt(left, right):
    return lax.dot_general(left, right, (((1,), (1,)), ((), ())), preferred_element_type=F32)


def mm_split(values, high, low):
    rows = values.shape[0]
    stacked = rows_of_halves(values)
    first = mm(stacked, high)
    second = mm(stacked[:rows], low)
    return first[:rows] + first[rows:] + second


def wide_node(points, coefs):
    first, second, third = poly_values(points)
    return 0.25 + 0.5 * (first * coefs[0] + second * coefs[1] + third * coefs[2])


def body(
    leaf_total,
    sub_total,
    coarse_levels,
    coords_hbm,
    vector_hbm,
    node_hbm,
    up_hbm,
    down_hbm,
    fine_hbm,
    coarse_hbm,
    out_ref,
    coords_ref,
    vector_ref,
    node_ref,
    up_ref,
    down_ref,
    pack,
    basis,
    flipped,
    near,
    near_out,
    mom,
    gathered,
    level_mom,
    fine_w,
    coarse_w,
    input_sem,
    weight_sem,
    coarse_sem,
    pack_send,
    pack_recv,
    mom_send,
    mom_recv,
    all_send,
    all_recv,
    partner_send,
    partner_recv,
    near_send,
    near_recv,
):
    leaf_at = lax.axis_index("leaf")
    sub_at = lax.axis_index("sub")
    rep_at = lax.axis_index("rep")
    me = leaf_at * sub_total + sub_at
    count = leaf_total * sub_total

    def peer(step):
        other = lax.rem(me + step, count)
        return other, {"leaf": other // sub_total, "sub": lax.rem(other, sub_total)}

    input_copies = [
        pltpu.make_async_copy(src, dst, input_sem.at[k])
        for k, (src, dst) in enumerate(
            (
                (coords_hbm, coords_ref),
                (vector_hbm, vector_ref),
                (node_hbm, node_ref),
                (up_hbm, up_ref),
                (down_hbm, down_ref),
            )
        )
    ]
    for copy in input_copies:
        copy.start()
    fine_copy = pltpu.make_async_copy(fine_hbm, fine_w, weight_sem)
    fine_copy.start()
    coarse_copies = []
    for pos in range(coarse_levels):
        row_bit = lax.rem(leaf_at // 2**pos, 2)
        col_bit = lax.rem(sub_at // 2**pos, 2)
        coarse_copies.append(
            pltpu.make_async_copy(
                coarse_hbm.at[pos, 2 * row_bit + col_bit], coarse_w.at[pos], coarse_sem.at[pos]
            )
        )
        coarse_copies[-1].start()

    empty = jnp.zeros((8, 256), F32)
    for k in range(SIDE + 2):
        for slot in range(2):
            pack[slot, 0, k] = empty
            pack[slot, SIDE + 1, k] = empty
            pack[slot, k, 0] = empty
            pack[slot, k, SIDE + 1] = empty
    for k in range(4):
        mom[0, k] = empty
        mom[3, k] = empty
        mom[k, 0] = empty
        mom[k, 3] = empty

    barrier = pltpu.get_barrier_semaphore()

    def greet(step, carry):
        at = lax.rem(2 * me + rep_at + step, 2 * count)
        other = at // 2
        where = {
            "leaf": other // sub_total,
            "sub": lax.rem(other, sub_total),
            "rep": lax.rem(at, 2),
        }
        pl.semaphore_signal(barrier, inc=1, device_id=where, device_id_type=MESH)
        return carry

    lax.fori_loop(1, 2 * count, greet, 0)

    input_copies[0].wait()
    input_copies[1].wait()
    row_start = (leaf_at * SIDE).astype(F32) + 0.5
    col_start = (sub_at * SIDE).astype(F32) + 0.5
    for i in range(SIDE):
        for j in range(SIDE):
            pack[0, i + 1, j + 1, 0:1] = coords_ref[0, i, j : j + 1] - (row_start + float(i))
            pack[0, i + 1, j + 1, 1:2] = coords_ref[1, i, j : j + 1] - (col_start + float(j))
            pack[0, i + 1, j + 1, 2:3] = coords_ref[2, i, j : j + 1] - 0.5
            pack[0, i + 1, j + 1, 3:4] = jnp.zeros((1, 256), F32)
            for c in range(4):
                pack[0, i + 1, j + 1, 4 + c : 5 + c] = vector_ref[c, i, j : j + 1]

    pl.semaphore_wait(barrier, 2 * count - 1)

    def edge(inner, shift):
        if shift == 0:
            return pl.ds(1, inner), pl.ds(1, inner)
        if shift < 0:
            return pl.ds(1, 1), pl.ds(inner + 1, 1)
        return pl.ds(inner, 1), pl.ds(0, 1)

    def halo(ref, inner, send, recv):
        copies = []
        for k, (di, dj) in enumerate(DIRECTIONS):
            src_i, dst_i = edge(inner, di)
            src_j, dst_j = edge(inner, dj)
            to_ok = (leaf_at + di >= 0) & (leaf_at + di < leaf_total)
            to_ok = to_ok & (sub_at + dj >= 0) & (sub_at + dj < sub_total)
            from_ok = (leaf_at - di >= 0) & (leaf_at - di < leaf_total)
            from_ok = from_ok & (sub_at - dj >= 0) & (sub_at - dj < sub_total)
            copy = pltpu.make_async_remote_copy(
                src_ref=ref.at[src_i, src_j],
                dst_ref=ref.at[dst_i, dst_j],
                send_sem=send.at[k],
                recv_sem=recv.at[k],
                device_id={"leaf": leaf_at + di, "sub": sub_at + dj},
                device_id_type=MESH,
            )
            copies.append((copy, to_ok, from_ok))
        for copy, to_ok, _ in copies:
            pl.when(to_ok)(copy.start)
        return copies

    def halo_wait(copies):
        for copy, to_ok, from_ok in copies:
            pl.when(to_ok)(copy.wait_send)
            pl.when(from_ok)(copy.wait_recv)

    partner_copy = pltpu.make_async_remote_copy(
        src_ref=pack.at[0, pl.ds(2 - rep_at, 3), pl.ds(1, SIDE)],
        dst_ref=pack.at[1, pl.ds(2 - rep_at, 3), pl.ds(1, SIDE)],
        send_sem=partner_send,
        recv_sem=partner_recv,
        device_id={"rep": 1 - rep_at},
        device_id_type=MESH,
    )
    partner_wait = pltpu.make_async_remote_copy(
        src_ref=pack.at[0, pl.ds(1 + rep_at, 3), pl.ds(1, SIDE)],
        dst_ref=pack.at[1, pl.ds(1 + rep_at, 3), pl.ds(1, SIDE)],
        send_sem=partner_send,
        recv_sem=partner_recv,
        device_id={"rep": 1 - rep_at},
        device_id_type=MESH,
    )
    pack_copies = []
    for k, (di, dj) in enumerate(DIRECTIONS):
        src_i, dst_i = edge(SIDE, di)
        src_j, dst_j = edge(SIDE, dj)
        to_ok = (leaf_at + di >= 0) & (leaf_at + di < leaf_total)
        to_ok = to_ok & (sub_at + dj >= 0) & (sub_at + dj < sub_total)
        from_ok = (leaf_at - di >= 0) & (leaf_at - di < leaf_total)
        from_ok = from_ok & (sub_at - dj >= 0) & (sub_at - dj < sub_total)
        for slot in range(2):
            to_rep = lax.rem(rep_at + slot, 2)
            goes, comes = to_ok, from_ok
            if di != 0:
                taker = 1 if di < 0 else 0
                goes = goes & (to_rep == taker)
                comes = comes & (rep_at == taker)
            copy = pltpu.make_async_remote_copy(
                src_ref=pack.at[0, src_i, src_j],
                dst_ref=pack.at[slot, dst_i, dst_j],
                send_sem=pack_send.at[k, slot],
                recv_sem=pack_recv.at[k, slot],
                device_id={"leaf": leaf_at + di, "sub": sub_at + dj, "rep": to_rep},
                device_id_type=MESH,
            )
            pack_copies.append((copy, goes, comes))
    for copy, goes, _ in pack_copies:
        pl.when(goes)(copy.start)
    partner_copy.start()

    nodes = np.array(poly_values(CHEB_NODES))
    for copy in input_copies[2:]:
        copy.wait()
    y_coefs = [node_ref[n] for n in range(3)]
    z_coefs = [node_ref[3 + n] for n in range(3)]
    row_id = lax.broadcasted_iota(jnp.int32, (8, 256), 0)
    for i in range(SIDE):
        for j in range(SIDE):
            box = pack[0, i + 1, j + 1]
            y_part = wide_node(2.0 * box[1:2], y_coefs)
            z_part = wide_node(2.0 * box[2:3], z_coefs)
            yz_part = y_part * z_part
            x_first = poly_values(2.0 * box[0:1])
            planes = []
            for k in range(4):
                weight = 0.25 + 0.5 * sum(x_first[n] * float(nodes[n, k]) for n in range(3))
                planes.append(yz_part * weight)
            wide = rows_of_halves(jnp.concatenate(planes, 0))
            basis[i * SIDE + j] = wide
            vec = box[4:8]
            v_high, v_low = halves(vec)
            both = jnp.concatenate([v_high, v_low, jnp.zeros((8, 256), F32)], 0).astype(BF16)
            got = mm_nt(both, wide)
            piece = got[0:4, 0:64] + got[4:8, 0:64] + got[0:4, 64:128]
            at = 64 * (2 * (i % 2) + j % 2)
            mom[1 + i // 2, 1 + j // 2, 0:4, at : at + 64] = piece
            mom[1 + i // 2, 1 + j // 2, 4:8, at : at + 64] = jnp.zeros((4, 64), F32)
    mom_copies = halo(mom, 2, mom_send, mom_recv)
    parents = jnp.concatenate([mom[1, 1], mom[1, 2], mom[2, 1], mom[2, 2]], 0)
    raised = mm_split(parents, up_ref[0], up_ref[1])
    gathered[me] = jnp.concatenate([raised[8 * k : 8 * k + 8] for k in range(4)], 1)

    def spread_copy(step, own_slot):
        other, where = peer(step)
        slot = me if own_slot else other
        return pltpu.make_async_remote_copy(
            src_ref=gathered.at[me],
            dst_ref=gathered.at[slot],
            send_sem=all_send.at[other],
            recv_sem=all_recv.at[slot],
            device_id=where,
            device_id_type=MESH,
        )

    def spread(step, carry):
        spread_copy(step, True).start()
        return carry

    lax.fori_loop(1, count, spread, 0)

    ones = jnp.ones((8, 256), F32)

    def parts_of(tile):
        first = tile.astype(BF16).astype(F32)
        rest = tile - first
        second = rest.astype(BF16).astype(F32)
        return first, second, rest - second

    def squares(tile):
        sq = tile * tile
        return sq[0:1] + sq[1:2] + sq[2:3]

    def flip(i, j):
        box = pack[0, i, j]
        first, second, third = parts_of(jnp.where(row_id < 3, box, 0.0))
        n_first, n_second, n_third = parts_of(squares(box))
        groups = []
        for norm in (n_first, n_second, n_third):
            tile = jnp.where(row_id == 3, ones, -2.0 * first)
            groups.append(jnp.where(row_id == 4, norm, tile))
        groups += [-2.0 * second, -2.0 * second, -2.0 * third]
        groups.append(jnp.zeros((80, 256), F32))
        flipped[i * (SIDE + 2) + j] = jnp.concatenate(groups, 0).T.astype(BF16)

    for k in range(3):
        for j in range(SIDE):
            flip(1 + rep_at + k, j + 1)
    halo_wait(pack_copies)
    partner_copy.wait_send()
    partner_wait.wait_recv()
    for j in range(SIDE + 2):
        flip(5 * rep_at, j)
    for k in range(3):
        flip(1 + rep_at + k, 0)
        flip(1 + rep_at + k, SIDE + 1)

    def near_box(box_at, carry):
        i = box_at // SIDE
        j = lax.rem(box_at, SIDE)
        target = pack[0, i + 1, j + 1]
        total = jnp.zeros((16, 256), F32)
        for di in range(3):
            for dj in range(3):
                moved = jnp.where(row_id == 0, target + float(1 - di), target)
                moved = jnp.where(row_id == 1, target + float(1 - dj), moved)
                norm = squares(moved) + SMOOTHING
                tile = jnp.where(row_id == 3, norm, jnp.where(row_id < 3, moved, 0.0))
                first, second, third = parts_of(tile)
                stacked = [
                    jnp.where(row_id == 4, ones, first),
                    jnp.where(row_id == 4, ones, second),
                    jnp.where(row_id == 4, ones, third),
                    first,
                    second,
                    first,
                ]
                feature = jnp.concatenate(stacked, 0).astype(BF16)
                vec = rows_of_halves(
                    jnp.concatenate(
                        [pack[0, i + di, j + dj, 4:8], pack[1, i + di, j + dj, 4:8]], 0
                    )
                )
                source = (i + di) * (SIDE + 2) + j + dj
                for half in range(2):
                    part = slice(128 * half, 128 * half + 128)
                    kern = lax.rsqrt(mm(flipped[source, part, :48], feature))
                    high = kern.astype(BF16)
                    low = (kern - high.astype(F32)).astype(BF16)
                    weights = jnp.concatenate([high, low], 0)
                    total = total + mm(jnp.concatenate([vec[:, part]] * 2, 1), weights)
        result = QUAD_WEIGHT * (total[0:8] + total[8:16])
        near[box_at] = result[0:4]
        near_out[box_at] = result[4:8]
        return carry

    def near_copy(row, step):
        at = pl.ds(SIDE * row, SIDE)
        return pltpu.make_async_remote_copy(
            src_ref=near_out.at[at],
            dst_ref=near.at[at],
            send_sem=near_send.at[step],
            recv_sem=near_recv.at[step],
            device_id={"rep": 1 - rep_at},
            device_id_type=MESH,
        )

    for step in range(2):
        row = 2 * rep_at + step
        lax.fori_loop(SIDE * row, SIDE * row + SIDE, near_box, 0)
        near_copy(row, step).start()

    def spread_wait(step, carry):
        spread_copy(step, True).wait_send()
        spread_copy(step, False).wait_recv()
        return carry

    lax.fori_loop(1, count, spread_wait, 0)

    def padded_read(row, col):
        row_ok = (row >= 0) & (row < leaf_total)
        col_ok = (col >= 0) & (col < sub_total)
        at = jnp.clip(row, 0, leaf_total - 1) * sub_total + jnp.clip(col, 0, sub_total - 1)
        return jnp.where(row_ok & col_ok, gathered[at], 0.0)

    for copy in coarse_copies:
        copy.wait()
    current = gathered[...].reshape(count * 8, 256)
    rows_here, cols_here = leaf_total, sub_total
    coarse_local = []
    for pos in range(coarse_levels):
        raised = mm_split(current, up_ref[0], up_ref[1])
        p_rows, p_cols = rows_here // 2, cols_here // 2
        for a in range(p_rows + 2):
            for b in range(p_cols + 2):
                if a in (0, p_rows + 1) or b in (0, p_cols + 1):
                    level_mom[pos, a, b] = empty
        tiles = []
        for a in range(p_rows):
            for b in range(p_cols):
                kids = []
                for d in range(2):
                    for e in range(2):
                        at = 8 * ((2 * a + d) * cols_here + 2 * b + e)
                        kids.append(raised[at : at + 8])
                tile = jnp.concatenate(kids, 1)
                level_mom[pos, a + 1, b + 1] = tile
                tiles.append(tile)
        pi = leaf_at // 2 ** (pos + 1)
        pj = sub_at // 2 ** (pos + 1)
        window = jnp.concatenate(
            [level_mom[pos, pi + a, pj + b] for a in range(3) for b in range(3)], 1
        )
        got = mm(rows_of_halves(window), coarse_w[pos])
        coarse_local.append(got[0:8, 0:64] + got[8:16, 0:64] + got[0:8, 64:128])
        current = jnp.concatenate(tiles, 0)
        rows_here, cols_here = p_rows, p_cols

    summed = coarse_local[-1]
    for pos in range(coarse_levels - 1, 0, -1):
        children = mm_split(summed, down_ref[0], down_ref[1])
        row_bit = lax.rem(leaf_at // 2 ** (pos - 1), 2)
        col_bit = lax.rem(sub_at // 2 ** (pos - 1), 2)
        child = 2 * row_bit + col_bit
        summed = coarse_local[pos - 1]
        for k in range(4):
            summed = summed + jnp.where(child == k, children[:, 64 * k : 64 * k + 64], 0.0)

    halo_wait(mom_copies)
    fine_copy.wait()
    window = jnp.concatenate(
        [padded_read(leaf_at + a, sub_at + b) for a in (-1, 0, 1) for b in (-1, 0, 1)], 1
    )
    level_one = mm_split(summed, down_ref[0], down_ref[1]) + mm_split(
        window, fine_w[1, 0], fine_w[1, 1]
    )
    stacked = jnp.concatenate([level_one[:, 64 * k : 64 * k + 64] for k in range(4)], 0)
    window = jnp.concatenate(
        [
            jnp.concatenate([mom[a + di, b + dj] for a in range(2) for b in range(2)], 0)
            for di in range(3)
            for dj in range(3)
        ],
        1,
    )
    level_zero = mm_split(stacked, down_ref[0], down_ref[1]) + mm_split(
        window, fine_w[0, 0], fine_w[0, 1]
    )
    for step in range(2):
        near_copy(2 * rep_at + step, step).wait_send()
        near_copy(2 - 2 * rep_at + step, step).wait_recv()
    for i in range(SIDE):
        for j in range(SIDE):
            row = 8 * (2 * (i // 2) + j // 2)
            at = 64 * (2 * (i % 2) + j % 2)
            coef = level_zero[row : row + 8, at : at + 64]
            high, low = halves(coef)
            wide = basis[i * SIDE + j]
            left = jnp.concatenate([high, low], 0).astype(BF16)
            got = mm(left, wide[:64])
            got_low = mm(left, wide[64:])
            result = near[i * SIDE + j] + got[0:4] + got[8:12] + got_low[0:4]
            for c in range(4):
                out_ref[c, i, j : j + 1] = result[c : c + 1]


def local(coords, vector):
    leaf_total = lax.axis_size("leaf")
    sub_total = lax.axis_size("sub")
    count = leaf_total * sub_total
    top_level = (SIDE * sub_total).bit_length() - 1
    coarse_levels = top_level - 2

    nodes = np.array(poly_values(CHEB_NODES))
    index = np.arange(16)
    node_table = np.concatenate([nodes[:, index // 4], nodes[:, index % 4]], 0)
    node_table = np.repeat(node_table[:, :, None], 256, 2).astype(np.float32)
    table = transfer_table()
    up = np.stack(halves_numpy(table.reshape(256, 64)))
    down = np.stack(halves_numpy(table.reshape(256, 64).T))
    fine = np.stack([np.stack(halves_numpy(parent_couplings(level))) for level in range(2)])
    coarse = []
    for level in range(2, top_level):
        high, low = halves_numpy(parent_couplings(level))
        high = high.reshape(2304, 4, 64).transpose(1, 0, 2)
        low = low.reshape(2304, 4, 64).transpose(1, 0, 2)
        coarse.append(np.concatenate([high, low], 2))
    coarse = np.stack(coarse)

    vmem = pl.BlockSpec(memory_space=pltpu.VMEM)
    hbm = pl.BlockSpec(memory_space=pltpu.HBM)
    dma = pltpu.SemaphoreType.DMA
    return pl.pallas_call(
        functools.partial(body, leaf_total, sub_total, coarse_levels),
        out_shape=jax.ShapeDtypeStruct(vector.shape, F32),
        in_specs=[hbm] * 7,
        out_specs=vmem,
        scratch_shapes=[
            pltpu.VMEM(coords.shape, F32),
            pltpu.VMEM(vector.shape, F32),
            pltpu.VMEM(node_table.shape, F32),
            pltpu.VMEM(up.shape, BF16),
            pltpu.VMEM(down.shape, BF16),
            pltpu.VMEM((2, SIDE + 2, SIDE + 2, 8, 256), F32),
            pltpu.VMEM((SIDE * SIDE, 128, 256), BF16),
            pltpu.VMEM(((SIDE + 2) ** 2, 256, 128), BF16),
            pltpu.VMEM((SIDE * SIDE, 4, 256), F32),
            pltpu.VMEM((SIDE * SIDE, 4, 256), F32),
            pltpu.VMEM((4, 4, 8, 256), F32),
            pltpu.VMEM((count, 8, 256), F32),
            pltpu.VMEM((coarse_levels, leaf_total // 2 + 2, sub_total // 2 + 2, 8, 256), F32),
            pltpu.VMEM((2, 2, 2304, 256), BF16),
            pltpu.VMEM((coarse_levels, 2304, 128), BF16),
            dma((5,)),
            dma,
            dma((coarse_levels,)),
            dma((8, 2)),
            dma((8, 2)),
            dma((8,)),
            dma((8,)),
            dma((count,)),
            dma((count,)),
            dma,
            dma,
            dma((2,)),
            dma((2,)),
        ],
        compiler_params=pltpu.CompilerParams(
            collective_id=0, has_side_effects=True, vmem_limit_bytes=60 * 1024 * 1024
        ),
    )(coords, vector, node_table, up, down, fine, coarse)


def solution(mesh):
    placed = (P(None, ("groups", "leaf"), "sub", None), P("rep", ("groups", "leaf"), "sub", None))
    return jax.shard_map(
        local,
        mesh=mesh,
        in_specs=placed,
        out_specs=P("rep", ("groups", "leaf"), "sub", None),
        check_vma=False,
    )
```

```python
import functools

import jax
import jax.numpy as jnp
import numpy as np
from jax import lax
from jax.experimental import pallas as pl
from jax.experimental.pallas import tpu as pltpu
from jax.sharding import PartitionSpec as P

QUAD_WEIGHT = 1.0 / 64.0
SMOOTHING = 0.01
CHEB_NODES = np.cos((2.0 * np.arange(4) + 1.0) * np.pi / 8.0)
SIDE = 4
F32 = jnp.float32
BF16 = jnp.bfloat16
MESH = pl.DeviceIdType.MESH
DIRECTIONS = [(-1, 0), (1, 0), (0, -1), (0, 1), (-1, -1), (-1, 1), (1, -1), (1, 1)]


def poly_values(points):
    second = 2.0 * points * points - 1.0
    third = 2.0 * points * second - points
    return (points, second, third)


def cheb_numpy(values):
    nodes_one, nodes_two, nodes_three = poly_values(CHEB_NODES)
    first, second, third = poly_values(values)
    return 0.25 + 0.5 * (
        first[..., None] * nodes_one
        + second[..., None] * nodes_two
        + third[..., None] * nodes_three
    )


def transfer_table():
    halves = [cheb_numpy((CHEB_NODES + 2.0 * side_bit - 1.0) / 2.0) for side_bit in range(2)]
    same_node = np.eye(4)
    blocks = [
        [
            (
                halves[row_bit][:, None, None, :, None, None]
                * halves[col_bit][None, :, None, None, :, None]
                * same_node[None, None, :, None, None, :]
            ).reshape(64, 64)
            for col_bit in range(2)
        ]
        for row_bit in range(2)
    ]
    return np.array(blocks)


def couple_table(tree_level):
    box_width = 2.0**tree_level
    across = 0.5 * box_width * CHEB_NODES
    height = 0.5 + 0.5 * CHEB_NODES
    target = np.stack(np.meshgrid(across, across, height, indexing="ij"), -1).reshape(64, 3)
    table_rows = []
    for row_shift in range(-3, 4):
        table_line = []
        for col_shift in range(-3, 4):
            source = target + np.array([row_shift * box_width, col_shift * box_width, 0.0])
            spacing = target[:, None, :] - source[None, :, :]
            values = QUAD_WEIGHT / np.sqrt(np.sum(spacing * spacing, -1) + SMOOTHING)
            far_flag = float(max(abs(row_shift), abs(col_shift)) >= 2)
            table_line.append(values * far_flag)
        table_rows.append(table_line)
    return np.array(table_rows)


def parent_couplings(tree_level):
    table = couple_table(tree_level).astype(np.float32)
    full = np.zeros((3, 3, 2, 2, 64, 2, 2, 64), np.float32)
    for pi in range(3):
        for pj in range(3):
            for sd in range(2):
                for se in range(2):
                    for td in range(2):
                        for te in range(2):
                            u = 2 * (pi - 1) + sd - td
                            v = 2 * (pj - 1) + se - te
                            full[pi, pj, sd, se, :, td, te, :] = table[u + 3, v + 3].T
    return full.reshape(2304, 256)


def halves_numpy(values):
    values = np.asarray(values, np.float32)
    high = values.astype(BF16)
    low = (values - high.astype(np.float32)).astype(BF16)
    return high, low


def halves(values):
    high = values.astype(BF16).astype(F32)
    return high, values - high


def rows_of_halves(values):
    high, low = halves(values)
    return jnp.concatenate([high, low], 0).astype(BF16)


def mm(left, right):
    return jnp.dot(left, right, preferred_element_type=F32)


def mm_nt(left, right):
    return lax.dot_general(left, right, (((1,), (1,)), ((), ())), preferred_element_type=F32)


def mm_split(values, high, low):
    rows = values.shape[0]
    stacked = rows_of_halves(values)
    first = mm(stacked, high)
    second = mm(stacked[:rows], low)
    return first[:rows] + first[rows:] + second


def wide_node(points, coefs):
    first, second, third = poly_values(points)
    return 0.25 + 0.5 * (first * coefs[0] + second * coefs[1] + third * coefs[2])


def body(
    leaf_total,
    sub_total,
    coarse_levels,
    coords_hbm,
    vector_hbm,
    node_hbm,
    up_hbm,
    down_hbm,
    fine_hbm,
    coarse_hbm,
    out_ref,
    coords_ref,
    vector_ref,
    node_ref,
    up_ref,
    down_ref,
    pack,
    basis,
    flipped,
    near,
    near_out,
    sums,
    mom,
    gathered,
    level_mom,
    fine_w,
    coarse_w,
    input_sem,
    weight_sem,
    coarse_sem,
    pack_send,
    pack_recv,
    mom_send,
    mom_recv,
    all_send,
    all_recv,
    partner_send,
    partner_recv,
    near_send,
    near_recv,
):
    leaf_at = lax.axis_index("leaf")
    sub_at = lax.axis_index("sub")
    rep_at = lax.axis_index("rep")
    me = leaf_at * sub_total + sub_at
    count = leaf_total * sub_total

    def peer(step):
        other = lax.rem(me + step, count)
        return other, {"leaf": other // sub_total, "sub": lax.rem(other, sub_total)}

    input_copies = [
        pltpu.make_async_copy(src, dst, input_sem.at[k])
        for k, (src, dst) in enumerate(
            (
                (coords_hbm, coords_ref),
                (vector_hbm, vector_ref),
                (node_hbm, node_ref),
                (up_hbm, up_ref),
                (down_hbm, down_ref),
            )
        )
    ]
    for copy in input_copies:
        copy.start()
    fine_copy = pltpu.make_async_copy(fine_hbm, fine_w, weight_sem)
    fine_copy.start()
    coarse_copies = []
    for pos in range(coarse_levels):
        row_bit = lax.rem(leaf_at // 2**pos, 2)
        col_bit = lax.rem(sub_at // 2**pos, 2)
        coarse_copies.append(
            pltpu.make_async_copy(
                coarse_hbm.at[pos, 2 * row_bit + col_bit], coarse_w.at[pos], coarse_sem.at[pos]
            )
        )
        coarse_copies[-1].start()

    empty = jnp.zeros((8, 256), F32)
    for k in range(SIDE + 2):
        for slot in range(2):
            pack[slot, 0, k] = empty
            pack[slot, SIDE + 1, k] = empty
            pack[slot, k, 0] = empty
            pack[slot, k, SIDE + 1] = empty
    for k in range(4):
        mom[0, k] = empty
        mom[3, k] = empty
        mom[k, 0] = empty
        mom[k, 3] = empty

    barrier = pltpu.get_barrier_semaphore()

    def greet(step, carry):
        at = lax.rem(2 * me + rep_at + step, 2 * count)
        other = at // 2
        where = {
            "leaf": other // sub_total,
            "sub": lax.rem(other, sub_total),
            "rep": lax.rem(at, 2),
        }
        pl.semaphore_signal(barrier, inc=1, device_id=where, device_id_type=MESH)
        return carry

    lax.fori_loop(1, 2 * count, greet, 0)

    input_copies[0].wait()
    input_copies[1].wait()
    row_start = (leaf_at * SIDE).astype(F32) + 0.5
    col_start = (sub_at * SIDE).astype(F32) + 0.5
    for i in range(SIDE):
        for j in range(SIDE):
            pack[0, i + 1, j + 1, 0:1] = coords_ref[0, i, j : j + 1] - (row_start + float(i))
            pack[0, i + 1, j + 1, 1:2] = coords_ref[1, i, j : j + 1] - (col_start + float(j))
            pack[0, i + 1, j + 1, 2:3] = coords_ref[2, i, j : j + 1] - 0.5
            pack[0, i + 1, j + 1, 3:4] = jnp.zeros((1, 256), F32)
            for c in range(4):
                pack[0, i + 1, j + 1, 4 + c : 5 + c] = vector_ref[c, i, j : j + 1]

    pl.semaphore_wait(barrier, 2 * count - 1)

    def edge(inner, shift):
        if shift == 0:
            return pl.ds(1, inner), pl.ds(1, inner)
        if shift < 0:
            return pl.ds(1, 1), pl.ds(inner + 1, 1)
        return pl.ds(inner, 1), pl.ds(0, 1)

    def halo(ref, inner, send, recv):
        copies = []
        for k, (di, dj) in enumerate(DIRECTIONS):
            src_i, dst_i = edge(inner, di)
            src_j, dst_j = edge(inner, dj)
            to_ok = (leaf_at + di >= 0) & (leaf_at + di < leaf_total)
            to_ok = to_ok & (sub_at + dj >= 0) & (sub_at + dj < sub_total)
            from_ok = (leaf_at - di >= 0) & (leaf_at - di < leaf_total)
            from_ok = from_ok & (sub_at - dj >= 0) & (sub_at - dj < sub_total)
            copy = pltpu.make_async_remote_copy(
                src_ref=ref.at[src_i, src_j],
                dst_ref=ref.at[dst_i, dst_j],
                send_sem=send.at[k],
                recv_sem=recv.at[k],
                device_id={"leaf": leaf_at + di, "sub": sub_at + dj},
                device_id_type=MESH,
            )
            copies.append((copy, to_ok, from_ok))
        for copy, to_ok, _ in copies:
            pl.when(to_ok)(copy.start)
        return copies

    def halo_wait(copies):
        for copy, to_ok, from_ok in copies:
            pl.when(to_ok)(copy.wait_send)
            pl.when(from_ok)(copy.wait_recv)

    partner_copy = pltpu.make_async_remote_copy(
        src_ref=pack.at[0, pl.ds(2 - rep_at, 3), pl.ds(1, SIDE)],
        dst_ref=pack.at[1, pl.ds(2 - rep_at, 3), pl.ds(1, SIDE)],
        send_sem=partner_send,
        recv_sem=partner_recv,
        device_id={"rep": 1 - rep_at},
        device_id_type=MESH,
    )
    partner_wait = pltpu.make_async_remote_copy(
        src_ref=pack.at[0, pl.ds(1 + rep_at, 3), pl.ds(1, SIDE)],
        dst_ref=pack.at[1, pl.ds(1 + rep_at, 3), pl.ds(1, SIDE)],
        send_sem=partner_send,
        recv_sem=partner_recv,
        device_id={"rep": 1 - rep_at},
        device_id_type=MESH,
    )
    pack_copies = []
    for k, (di, dj) in enumerate(DIRECTIONS):
        src_i, dst_i = edge(SIDE, di)
        src_j, dst_j = edge(SIDE, dj)
        to_ok = (leaf_at + di >= 0) & (leaf_at + di < leaf_total)
        to_ok = to_ok & (sub_at + dj >= 0) & (sub_at + dj < sub_total)
        from_ok = (leaf_at - di >= 0) & (leaf_at - di < leaf_total)
        from_ok = from_ok & (sub_at - dj >= 0) & (sub_at - dj < sub_total)
        for slot in range(2):
            to_rep = lax.rem(rep_at + slot, 2)
            goes, comes = to_ok, from_ok
            if di != 0:
                taker = 1 if di < 0 else 0
                goes = goes & (to_rep == taker)
                comes = comes & (rep_at == taker)
            copy = pltpu.make_async_remote_copy(
                src_ref=pack.at[0, src_i, src_j],
                dst_ref=pack.at[slot, dst_i, dst_j],
                send_sem=pack_send.at[k, slot],
                recv_sem=pack_recv.at[k, slot],
                device_id={"leaf": leaf_at + di, "sub": sub_at + dj, "rep": to_rep},
                device_id_type=MESH,
            )
            pack_copies.append((copy, goes, comes))
    for copy, goes, _ in pack_copies:
        pl.when(goes)(copy.start)
    partner_copy.start()

    nodes = np.array(poly_values(CHEB_NODES))
    for copy in input_copies[2:]:
        copy.wait()
    y_coefs = [node_ref[n] for n in range(3)]
    z_coefs = [node_ref[3 + n] for n in range(3)]
    row_id = lax.broadcasted_iota(jnp.int32, (8, 256), 0)
    for i in range(SIDE):
        for j in range(SIDE):
            box = pack[0, i + 1, j + 1]
            y_part = wide_node(2.0 * box[1:2], y_coefs)
            z_part = wide_node(2.0 * box[2:3], z_coefs)
            yz_part = y_part * z_part
            x_first = poly_values(2.0 * box[0:1])
            planes = []
            for k in range(4):
                weight = 0.25 + 0.5 * sum(x_first[n] * float(nodes[n, k]) for n in range(3))
                planes.append(yz_part * weight)
            wide = rows_of_halves(jnp.concatenate(planes, 0))
            basis[i * SIDE + j] = wide
            vec = box[4:8]
            v_high, v_low = halves(vec)
            both = jnp.concatenate([v_high, v_low, jnp.zeros((8, 256), F32)], 0).astype(BF16)
            got = mm_nt(both, wide)
            piece = got[0:4, 0:64] + got[4:8, 0:64] + got[0:4, 64:128]
            at = 64 * (2 * (i % 2) + j % 2)
            mom[1 + i // 2, 1 + j // 2, 0:4, at : at + 64] = piece
            mom[1 + i // 2, 1 + j // 2, 4:8, at : at + 64] = jnp.zeros((4, 64), F32)
    mom_copies = halo(mom, 2, mom_send, mom_recv)
    parents = jnp.concatenate([mom[1, 1], mom[1, 2], mom[2, 1], mom[2, 2]], 0)
    raised = mm_split(parents, up_ref[0], up_ref[1])
    gathered[me] = jnp.concatenate([raised[8 * k : 8 * k + 8] for k in range(4)], 1)

    def spread_copy(step, own_slot):
        other, where = peer(step)
        slot = me if own_slot else other
        return pltpu.make_async_remote_copy(
            src_ref=gathered.at[me],
            dst_ref=gathered.at[slot],
            send_sem=all_send.at[other],
            recv_sem=all_recv.at[slot],
            device_id=where,
            device_id_type=MESH,
        )

    def spread(step, carry):
        spread_copy(step, True).start()
        return carry

    lax.fori_loop(1, count, spread, 0)

    ones = jnp.ones((8, 256), F32)

    def parts_of(tile):
        first = tile.astype(BF16).astype(F32)
        rest = tile - first
        second = rest.astype(BF16).astype(F32)
        return first, second, rest - second

    def squares(tile):
        sq = tile * tile
        return sq[0:1] + sq[1:2] + sq[2:3]

    def flip(i, j):
        box = pack[0, i, j]
        first, second, third = parts_of(jnp.where(row_id < 3, box, 0.0))
        n_first, n_second, n_third = parts_of(squares(box))
        groups = []
        for norm in (n_first, n_second, n_third):
            tile = jnp.where(row_id == 3, ones, -2.0 * first)
            groups.append(jnp.where(row_id == 4, norm, tile))
        groups += [-2.0 * second, -2.0 * second, -2.0 * third]
        groups.append(jnp.zeros((80, 256), F32))
        flipped[i * (SIDE + 2) + j] = jnp.concatenate(groups, 0).T.astype(BF16)

    for k in range(3):
        for j in range(SIDE):
            flip(1 + rep_at + k, j + 1)
    partner_copy.wait_send()
    partner_wait.wait_recv()

    def pair(i, j, row, col):
        target = pack[0, i + 1, j + 1]
        moved = jnp.where(row_id == 0, target + (i + 1 - row).astype(F32), target)
        moved = jnp.where(row_id == 1, target + float(j + 1 - col), moved)
        norm = squares(moved) + SMOOTHING
        tile = jnp.where(row_id == 3, norm, jnp.where(row_id < 3, moved, 0.0))
        first, second, third = parts_of(tile)
        stacked = [
            jnp.where(row_id == 4, ones, first),
            jnp.where(row_id == 4, ones, second),
            jnp.where(row_id == 4, ones, third),
            first,
            second,
            first,
        ]
        feature = jnp.concatenate(stacked, 0).astype(BF16)
        vec = rows_of_halves(
            jnp.concatenate([pack[0, row, col, 4:8], pack[1, row, col, 4:8]], 0)
        )
        source = row * (SIDE + 2) + col
        total = jnp.zeros((16, 256), F32)
        for half in range(2):
            part = slice(128 * half, 128 * half + 128)
            kern = lax.rsqrt(mm(flipped[source, part, :48], feature))
            high = kern.astype(BF16)
            low = (kern - high.astype(F32)).astype(BF16)
            weights = jnp.concatenate([high, low], 0)
            total = total + mm(jnp.concatenate([vec[:, part]] * 2, 1), weights)
        return total

    def own_rows(t):
        outer = t // 3
        i = outer * 3 * rep_at + (1 - outer) * (1 + rep_at)
        row = outer * (1 + 2 * rep_at + t - 3) + (1 - outer) * (1 + rep_at + t)
        step = (outer + 1 + rep_at) % 2
        return i, row, step

    for k in range(2):
        for j in range(SIDE):
            sums[k, j] = jnp.zeros((16, 256), F32)

    def own_pairs(t, carry):
        i, row, step = own_rows(t)
        for j in range(SIDE):
            total = sums[step, j]
            for col in range(max(j, 1), min(j + 3, SIDE + 1)):
                total = total + pair(i, j, row, col)
            sums[step, j] = total
        return carry

    lax.fori_loop(0, 5, own_pairs, 0)
    halo_wait(pack_copies)
    for j in range(SIDE + 2):
        flip(5 * rep_at, j)
    for k in range(3):
        flip(1 + rep_at + k, 0)
        flip(1 + rep_at + k, SIDE + 1)

    def side_pairs(t, carry):
        i, row, step = own_rows(t)
        sums[step, 0] += pair(i, 0, row, 0)
        sums[step, SIDE - 1] += pair(i, SIDE - 1, row, SIDE + 1)
        return carry

    lax.fori_loop(0, 5, side_pairs, 0)
    for j in range(SIDE):
        total = sums[rep_at, j]
        for col in range(j, j + 3):
            total = total + pair(3 * rep_at, j, 5 * rep_at, col)
        sums[rep_at, j] = total

    def near_copy(row, step):
        at = pl.ds(SIDE * row, SIDE)
        return pltpu.make_async_remote_copy(
            src_ref=near_out.at[at],
            dst_ref=near.at[at],
            send_sem=near_send.at[step],
            recv_sem=near_recv.at[step],
            device_id={"rep": 1 - rep_at},
            device_id_type=MESH,
        )

    for step in range(2):
        row = 2 * rep_at + step
        for j in range(SIDE):
            total = sums[step, j]
            result = QUAD_WEIGHT * (total[0:8] + total[8:16])
            near[SIDE * row + j] = result[0:4]
            near_out[SIDE * row + j] = result[4:8]
        near_copy(row, step).start()

    def spread_wait(step, carry):
        spread_copy(step, True).wait_send()
        spread_copy(step, False).wait_recv()
        return carry

    lax.fori_loop(1, count, spread_wait, 0)

    def padded_read(row, col):
        row_ok = (row >= 0) & (row < leaf_total)
        col_ok = (col >= 0) & (col < sub_total)
        at = jnp.clip(row, 0, leaf_total - 1) * sub_total + jnp.clip(col, 0, sub_total - 1)
        return jnp.where(row_ok & col_ok, gathered[at], 0.0)

    for copy in coarse_copies:
        copy.wait()
    current = gathered[...].reshape(count * 8, 256)
    rows_here, cols_here = leaf_total, sub_total
    coarse_local = []
    for pos in range(coarse_levels):
        raised = mm_split(current, up_ref[0], up_ref[1])
        p_rows, p_cols = rows_here // 2, cols_here // 2
        for a in range(p_rows + 2):
            for b in range(p_cols + 2):
                if a in (0, p_rows + 1) or b in (0, p_cols + 1):
                    level_mom[pos, a, b] = empty
        tiles = []
        for a in range(p_rows):
            for b in range(p_cols):
                kids = []
                for d in range(2):
                    for e in range(2):
                        at = 8 * ((2 * a + d) * cols_here + 2 * b + e)
                        kids.append(raised[at : at + 8])
                tile = jnp.concatenate(kids, 1)
                level_mom[pos, a + 1, b + 1] = tile
                tiles.append(tile)
        pi = leaf_at // 2 ** (pos + 1)
        pj = sub_at // 2 ** (pos + 1)
        window = jnp.concatenate(
            [level_mom[pos, pi + a, pj + b] for a in range(3) for b in range(3)], 1
        )
        got = mm(rows_of_halves(window), coarse_w[pos])
        coarse_local.append(got[0:8, 0:64] + got[8:16, 0:64] + got[0:8, 64:128])
        current = jnp.concatenate(tiles, 0)
        rows_here, cols_here = p_rows, p_cols

    summed = coarse_local[-1]
    for pos in range(coarse_levels - 1, 0, -1):
        children = mm_split(summed, down_ref[0], down_ref[1])
        row_bit = lax.rem(leaf_at // 2 ** (pos - 1), 2)
        col_bit = lax.rem(sub_at // 2 ** (pos - 1), 2)
        child = 2 * row_bit + col_bit
        summed = coarse_local[pos - 1]
        for k in range(4):
            summed = summed + jnp.where(child == k, children[:, 64 * k : 64 * k + 64], 0.0)

    halo_wait(mom_copies)
    fine_copy.wait()
    window = jnp.concatenate(
        [padded_read(leaf_at + a, sub_at + b) for a in (-1, 0, 1) for b in (-1, 0, 1)], 1
    )
    level_one = mm_split(summed, down_ref[0], down_ref[1]) + mm_split(
        window, fine_w[1, 0], fine_w[1, 1]
    )
    stacked = jnp.concatenate([level_one[:, 64 * k : 64 * k + 64] for k in range(4)], 0)
    window = jnp.concatenate(
        [
            jnp.concatenate([mom[a + di, b + dj] for a in range(2) for b in range(2)], 0)
            for di in range(3)
            for dj in range(3)
        ],
        1,
    )
    level_zero = mm_split(stacked, down_ref[0], down_ref[1]) + mm_split(
        window, fine_w[0, 0], fine_w[0, 1]
    )
    for step in range(2):
        near_copy(2 * rep_at + step, step).wait_send()
        near_copy(2 - 2 * rep_at + step, step).wait_recv()
    for i in range(SIDE):
        for j in range(SIDE):
            row = 8 * (2 * (i // 2) + j // 2)
            at = 64 * (2 * (i % 2) + j % 2)
            coef = level_zero[row : row + 8, at : at + 64]
            high, low = halves(coef)
            wide = basis[i * SIDE + j]
            left = jnp.concatenate([high, low], 0).astype(BF16)
            got = mm(left, wide[:64])
            got_low = mm(left, wide[64:])
            result = near[i * SIDE + j] + got[0:4] + got[8:12] + got_low[0:4]
            for c in range(4):
                out_ref[c, i, j : j + 1] = result[c : c + 1]


def local(coords, vector):
    leaf_total = lax.axis_size("leaf")
    sub_total = lax.axis_size("sub")
    count = leaf_total * sub_total
    top_level = (SIDE * sub_total).bit_length() - 1
    coarse_levels = top_level - 2

    nodes = np.array(poly_values(CHEB_NODES))
    index = np.arange(16)
    node_table = np.concatenate([nodes[:, index // 4], nodes[:, index % 4]], 0)
    node_table = np.repeat(node_table[:, :, None], 256, 2).astype(np.float32)
    table = transfer_table()
    up = np.stack(halves_numpy(table.reshape(256, 64)))
    down = np.stack(halves_numpy(table.reshape(256, 64).T))
    fine = np.stack([np.stack(halves_numpy(parent_couplings(level))) for level in range(2)])
    coarse = []
    for level in range(2, top_level):
        high, low = halves_numpy(parent_couplings(level))
        high = high.reshape(2304, 4, 64).transpose(1, 0, 2)
        low = low.reshape(2304, 4, 64).transpose(1, 0, 2)
        coarse.append(np.concatenate([high, low], 2))
    coarse = np.stack(coarse)

    vmem = pl.BlockSpec(memory_space=pltpu.VMEM)
    hbm = pl.BlockSpec(memory_space=pltpu.HBM)
    dma = pltpu.SemaphoreType.DMA
    return pl.pallas_call(
        functools.partial(body, leaf_total, sub_total, coarse_levels),
        out_shape=jax.ShapeDtypeStruct(vector.shape, F32),
        in_specs=[hbm] * 7,
        out_specs=vmem,
        scratch_shapes=[
            pltpu.VMEM(coords.shape, F32),
            pltpu.VMEM(vector.shape, F32),
            pltpu.VMEM(node_table.shape, F32),
            pltpu.VMEM(up.shape, BF16),
            pltpu.VMEM(down.shape, BF16),
            pltpu.VMEM((2, SIDE + 2, SIDE + 2, 8, 256), F32),
            pltpu.VMEM((SIDE * SIDE, 128, 256), BF16),
            pltpu.VMEM(((SIDE + 2) ** 2, 256, 128), BF16),
            pltpu.VMEM((SIDE * SIDE, 4, 256), F32),
            pltpu.VMEM((SIDE * SIDE, 4, 256), F32),
            pltpu.VMEM((2, SIDE, 16, 256), F32),
            pltpu.VMEM((4, 4, 8, 256), F32),
            pltpu.VMEM((count, 8, 256), F32),
            pltpu.VMEM((coarse_levels, leaf_total // 2 + 2, sub_total // 2 + 2, 8, 256), F32),
            pltpu.VMEM((2, 2, 2304, 256), BF16),
            pltpu.VMEM((coarse_levels, 2304, 128), BF16),
            dma((5,)),
            dma,
            dma((coarse_levels,)),
            dma((8, 2)),
            dma((8, 2)),
            dma((8,)),
            dma((8,)),
            dma((count,)),
            dma((count,)),
            dma,
            dma,
            dma((2,)),
            dma((2,)),
        ],
        compiler_params=pltpu.CompilerParams(
            collective_id=0, has_side_effects=True, vmem_limit_bytes=60 * 1024 * 1024
        ),
    )(coords, vector, node_table, up, down, fine, coarse)


def solution(mesh):
    placed = (P(None, ("groups", "leaf"), "sub", None), P("rep", ("groups", "leaf"), "sub", None))
    return jax.shard_map(
        local,
        mesh=mesh,
        in_specs=placed,
        out_specs=P("rep", ("groups", "leaf"), "sub", None),
        check_vma=False,
    )
```

```python
import functools

import jax
import jax.numpy as jnp
import numpy as np
from jax import lax
from jax.experimental import pallas as pl
from jax.experimental.pallas import tpu as pltpu
from jax.sharding import PartitionSpec as P

QUAD_WEIGHT = 1.0 / 64.0
SMOOTHING = 0.01
CHEB_NODES = np.cos((2.0 * np.arange(4) + 1.0) * np.pi / 8.0)
SIDE = 4
F32 = jnp.float32
BF16 = jnp.bfloat16
MESH = pl.DeviceIdType.MESH
DIRECTIONS = [(-1, 0), (1, 0), (0, -1), (0, 1), (-1, -1), (-1, 1), (1, -1), (1, 1)]


def poly_values(points):
    second = 2.0 * points * points - 1.0
    third = 2.0 * points * second - points
    return (points, second, third)


def cheb_numpy(values):
    nodes_one, nodes_two, nodes_three = poly_values(CHEB_NODES)
    first, second, third = poly_values(values)
    return 0.25 + 0.5 * (
        first[..., None] * nodes_one
        + second[..., None] * nodes_two
        + third[..., None] * nodes_three
    )


def transfer_table():
    halves = [cheb_numpy((CHEB_NODES + 2.0 * side_bit - 1.0) / 2.0) for side_bit in range(2)]
    same_node = np.eye(4)
    blocks = [
        [
            (
                halves[row_bit][:, None, None, :, None, None]
                * halves[col_bit][None, :, None, None, :, None]
                * same_node[None, None, :, None, None, :]
            ).reshape(64, 64)
            for col_bit in range(2)
        ]
        for row_bit in range(2)
    ]
    return np.array(blocks)


def couple_table(tree_level):
    box_width = 2.0**tree_level
    across = 0.5 * box_width * CHEB_NODES
    height = 0.5 + 0.5 * CHEB_NODES
    target = np.stack(np.meshgrid(across, across, height, indexing="ij"), -1).reshape(64, 3)
    table_rows = []
    for row_shift in range(-3, 4):
        table_line = []
        for col_shift in range(-3, 4):
            source = target + np.array([row_shift * box_width, col_shift * box_width, 0.0])
            spacing = target[:, None, :] - source[None, :, :]
            values = QUAD_WEIGHT / np.sqrt(np.sum(spacing * spacing, -1) + SMOOTHING)
            far_flag = float(max(abs(row_shift), abs(col_shift)) >= 2)
            table_line.append(values * far_flag)
        table_rows.append(table_line)
    return np.array(table_rows)


def parent_couplings(tree_level):
    table = couple_table(tree_level).astype(np.float32)
    full = np.zeros((3, 3, 2, 2, 64, 2, 2, 64), np.float32)
    for pi in range(3):
        for pj in range(3):
            for sd in range(2):
                for se in range(2):
                    for td in range(2):
                        for te in range(2):
                            u = 2 * (pi - 1) + sd - td
                            v = 2 * (pj - 1) + se - te
                            full[pi, pj, sd, se, :, td, te, :] = table[u + 3, v + 3].T
    return full.reshape(2304, 256)


def halves_numpy(values):
    values = np.asarray(values, np.float32)
    high = values.astype(BF16)
    low = (values - high.astype(np.float32)).astype(BF16)
    return high, low


def halves(values):
    high = values.astype(BF16).astype(F32)
    return high, values - high


def rows_of_halves(values):
    high, low = halves(values)
    return jnp.concatenate([high, low], 0).astype(BF16)


def mm(left, right):
    return jnp.dot(left, right, preferred_element_type=F32)


def mm_nt(left, right):
    return lax.dot_general(left, right, (((1,), (1,)), ((), ())), preferred_element_type=F32)


def mm_split(values, high, low):
    rows = values.shape[0]
    stacked = rows_of_halves(values)
    first = mm(stacked, high)
    second = mm(stacked[:rows], low)
    return first[:rows] + first[rows:] + second


def wide_node(points, coefs):
    first, second, third = poly_values(points)
    return 0.25 + 0.5 * (first * coefs[0] + second * coefs[1] + third * coefs[2])


def body(
    leaf_total,
    sub_total,
    coarse_levels,
    coords_hbm,
    vector_hbm,
    node_hbm,
    up_hbm,
    down_hbm,
    fine_hbm,
    coarse_hbm,
    out_ref,
    coords_ref,
    vector_ref,
    node_ref,
    up_ref,
    down_ref,
    pack,
    basis,
    flipped,
    near,
    near_out,
    sums,
    mom,
    gathered,
    level_mom,
    fine_w,
    coarse_w,
    input_sem,
    weight_sem,
    coarse_sem,
    pack_send,
    pack_recv,
    mom_send,
    mom_recv,
    all_send,
    all_recv,
    partner_send,
    partner_recv,
    near_send,
    near_recv,
):
    leaf_at = lax.axis_index("leaf")
    sub_at = lax.axis_index("sub")
    rep_at = lax.axis_index("rep")
    me = leaf_at * sub_total + sub_at
    count = leaf_total * sub_total

    def peer(step):
        other = lax.rem(me + step, count)
        return other, {"leaf": other // sub_total, "sub": lax.rem(other, sub_total)}

    input_copies = [
        pltpu.make_async_copy(src, dst, input_sem.at[k])
        for k, (src, dst) in enumerate(
            (
                (coords_hbm, coords_ref),
                (vector_hbm, vector_ref),
                (node_hbm, node_ref),
                (up_hbm, up_ref),
                (down_hbm, down_ref),
            )
        )
    ]
    for copy in input_copies:
        copy.start()
    fine_copy = pltpu.make_async_copy(fine_hbm, fine_w, weight_sem)
    fine_copy.start()
    coarse_copies = []
    for pos in range(coarse_levels):
        row_bit = lax.rem(leaf_at // 2**pos, 2)
        col_bit = lax.rem(sub_at // 2**pos, 2)
        coarse_copies.append(
            pltpu.make_async_copy(
                coarse_hbm.at[pos, 2 * row_bit + col_bit], coarse_w.at[pos], coarse_sem.at[pos]
            )
        )
        coarse_copies[-1].start()

    empty = jnp.zeros((8, 256), F32)
    for k in range(SIDE + 2):
        for slot in range(2):
            pack[slot, 0, k] = empty
            pack[slot, SIDE + 1, k] = empty
            pack[slot, k, 0] = empty
            pack[slot, k, SIDE + 1] = empty
    for k in range(4):
        mom[0, k] = empty
        mom[3, k] = empty
        mom[k, 0] = empty
        mom[k, 3] = empty

    barrier = pltpu.get_barrier_semaphore()

    def greet(step, carry):
        at = lax.rem(2 * me + rep_at + step, 2 * count)
        other = at // 2
        where = {
            "leaf": other // sub_total,
            "sub": lax.rem(other, sub_total),
            "rep": lax.rem(at, 2),
        }
        pl.semaphore_signal(barrier, inc=1, device_id=where, device_id_type=MESH)
        return carry

    lax.fori_loop(1, 2 * count, greet, 0)

    input_copies[0].wait()
    input_copies[1].wait()
    row_start = (leaf_at * SIDE).astype(F32) + 0.5
    col_start = (sub_at * SIDE).astype(F32) + 0.5
    for i in range(SIDE):
        for j in range(SIDE):
            pack[0, i + 1, j + 1, 0:1] = coords_ref[0, i, j : j + 1] - (row_start + float(i))
            pack[0, i + 1, j + 1, 1:2] = coords_ref[1, i, j : j + 1] - (col_start + float(j))
            pack[0, i + 1, j + 1, 2:3] = coords_ref[2, i, j : j + 1] - 0.5
            pack[0, i + 1, j + 1, 3:4] = jnp.zeros((1, 256), F32)
            for c in range(4):
                pack[0, i + 1, j + 1, 4 + c : 5 + c] = vector_ref[c, i, j : j + 1]

    pl.semaphore_wait(barrier, 2 * count - 1)

    def edge(inner, shift):
        if shift == 0:
            return pl.ds(1, inner), pl.ds(1, inner)
        if shift < 0:
            return pl.ds(1, 1), pl.ds(inner + 1, 1)
        return pl.ds(inner, 1), pl.ds(0, 1)

    def halo(ref, inner, send, recv):
        copies = []
        for k, (di, dj) in enumerate(DIRECTIONS):
            src_i, dst_i = edge(inner, di)
            src_j, dst_j = edge(inner, dj)
            to_ok = (leaf_at + di >= 0) & (leaf_at + di < leaf_total)
            to_ok = to_ok & (sub_at + dj >= 0) & (sub_at + dj < sub_total)
            from_ok = (leaf_at - di >= 0) & (leaf_at - di < leaf_total)
            from_ok = from_ok & (sub_at - dj >= 0) & (sub_at - dj < sub_total)
            copy = pltpu.make_async_remote_copy(
                src_ref=ref.at[src_i, src_j],
                dst_ref=ref.at[dst_i, dst_j],
                send_sem=send.at[k],
                recv_sem=recv.at[k],
                device_id={"leaf": leaf_at + di, "sub": sub_at + dj},
                device_id_type=MESH,
            )
            copies.append((copy, to_ok, from_ok))
        for copy, to_ok, _ in copies:
            pl.when(to_ok)(copy.start)
        return copies

    def halo_wait(copies):
        for copy, to_ok, from_ok in copies:
            pl.when(to_ok)(copy.wait_send)
            pl.when(from_ok)(copy.wait_recv)

    partner_copy = pltpu.make_async_remote_copy(
        src_ref=pack.at[0, pl.ds(2 - rep_at, 3), pl.ds(1, SIDE)],
        dst_ref=pack.at[1, pl.ds(2 - rep_at, 3), pl.ds(1, SIDE)],
        send_sem=partner_send,
        recv_sem=partner_recv,
        device_id={"rep": 1 - rep_at},
        device_id_type=MESH,
    )
    partner_wait = pltpu.make_async_remote_copy(
        src_ref=pack.at[0, pl.ds(1 + rep_at, 3), pl.ds(1, SIDE)],
        dst_ref=pack.at[1, pl.ds(1 + rep_at, 3), pl.ds(1, SIDE)],
        send_sem=partner_send,
        recv_sem=partner_recv,
        device_id={"rep": 1 - rep_at},
        device_id_type=MESH,
    )
    partner_copy.start()
    pack_copies = []
    for k, (di, dj) in enumerate(DIRECTIONS):
        src_i, dst_i = edge(SIDE, di)
        src_j, dst_j = edge(SIDE, dj)
        to_ok = (leaf_at + di >= 0) & (leaf_at + di < leaf_total)
        to_ok = to_ok & (sub_at + dj >= 0) & (sub_at + dj < sub_total)
        from_ok = (leaf_at - di >= 0) & (leaf_at - di < leaf_total)
        from_ok = from_ok & (sub_at - dj >= 0) & (sub_at - dj < sub_total)
        for slot in range(2):
            to_rep = lax.rem(rep_at + slot, 2)
            goes, comes = to_ok, from_ok
            if di != 0:
                taker = 1 if di < 0 else 0
                goes = goes & (to_rep == taker)
                comes = comes & (rep_at == taker)
            copy = pltpu.make_async_remote_copy(
                src_ref=pack.at[0, src_i, src_j],
                dst_ref=pack.at[slot, dst_i, dst_j],
                send_sem=pack_send.at[k, slot],
                recv_sem=pack_recv.at[k, slot],
                device_id={"leaf": leaf_at + di, "sub": sub_at + dj, "rep": to_rep},
                device_id_type=MESH,
            )
            pack_copies.append((copy, goes, comes))
    for copy, goes, _ in pack_copies:
        pl.when(goes)(copy.start)

    nodes = np.array(poly_values(CHEB_NODES))
    for copy in input_copies[2:]:
        copy.wait()
    y_coefs = [node_ref[n] for n in range(3)]
    z_coefs = [node_ref[3 + n] for n in range(3)]
    row_id = lax.broadcasted_iota(jnp.int32, (8, 256), 0)
    for i in range(SIDE):
        for j in range(SIDE):
            box = pack[0, i + 1, j + 1]
            y_part = wide_node(2.0 * box[1:2], y_coefs)
            z_part = wide_node(2.0 * box[2:3], z_coefs)
            yz_part = y_part * z_part
            x_first = poly_values(2.0 * box[0:1])
            planes = []
            for k in range(4):
                weight = 0.25 + 0.5 * sum(x_first[n] * float(nodes[n, k]) for n in range(3))
                planes.append(yz_part * weight)
            wide = rows_of_halves(jnp.concatenate(planes, 0))
            basis[i * SIDE + j] = wide
            vec = box[4:8]
            v_high, v_low = halves(vec)
            both = jnp.concatenate([v_high, v_low, jnp.zeros((8, 256), F32)], 0).astype(BF16)
            got = mm_nt(both, wide)
            piece = got[0:4, 0:64] + got[4:8, 0:64] + got[0:4, 64:128]
            at = 64 * (2 * (i % 2) + j % 2)
            mom[1 + i // 2, 1 + j // 2, 0:4, at : at + 64] = piece
            mom[1 + i // 2, 1 + j // 2, 4:8, at : at + 64] = jnp.zeros((4, 64), F32)
    mom_copies = halo(mom, 2, mom_send, mom_recv)
    parents = jnp.concatenate([mom[1, 1], mom[1, 2], mom[2, 1], mom[2, 2]], 0)
    raised = mm_split(parents, up_ref[0], up_ref[1])
    gathered[me] = jnp.concatenate([raised[8 * k : 8 * k + 8] for k in range(4)], 1)

    def spread_copy(step, own_slot):
        other, where = peer(step)
        slot = me if own_slot else other
        return pltpu.make_async_remote_copy(
            src_ref=gathered.at[me],
            dst_ref=gathered.at[slot],
            send_sem=all_send.at[other],
            recv_sem=all_recv.at[slot],
            device_id=where,
            device_id_type=MESH,
        )

    def spread(step, carry):
        spread_copy(step, True).start()
        return carry

    lax.fori_loop(1, count, spread, 0)

    ones = jnp.ones((8, 256), F32)

    def parts_of(tile):
        first = tile.astype(BF16).astype(F32)
        rest = tile - first
        second = rest.astype(BF16).astype(F32)
        return first, second, rest - second

    def squares(tile):
        sq = tile * tile
        return sq[0:1] + sq[1:2] + sq[2:3]

    def flip(i, j):
        box = pack[0, i, j]
        first, second, third = parts_of(jnp.where(row_id < 3, box, 0.0))
        n_first, n_second, n_third = parts_of(squares(box))
        groups = []
        for norm in (n_first, n_second, n_third):
            tile = jnp.where(row_id == 3, ones, -2.0 * first)
            groups.append(jnp.where(row_id == 4, norm, tile))
        groups += [-2.0 * second, -2.0 * second, -2.0 * third]
        groups.append(jnp.zeros((80, 256), F32))
        flipped[i * (SIDE + 2) + j] = jnp.concatenate(groups, 0).T.astype(BF16)

    for k in range(3):
        for j in range(SIDE):
            flip(1 + rep_at + k, j + 1)
    partner_copy.wait_send()
    partner_wait.wait_recv()

    def pair(i, j, row, col):
        target = pack[0, i + 1, j + 1]
        moved = jnp.where(row_id == 0, target + (i + 1 - row).astype(F32), target)
        moved = jnp.where(row_id == 1, target + float(j + 1 - col), moved)
        norm = squares(moved) + SMOOTHING
        tile = jnp.where(row_id == 3, norm, jnp.where(row_id < 3, moved, 0.0))
        first, second, third = parts_of(tile)
        stacked = [
            jnp.where(row_id == 4, ones, first),
            jnp.where(row_id == 4, ones, second),
            jnp.where(row_id == 4, ones, third),
            first,
            second,
            first,
        ]
        feature = jnp.concatenate(stacked, 0).astype(BF16)
        vec = rows_of_halves(
            jnp.concatenate([pack[0, row, col, 4:8], pack[1, row, col, 4:8]], 0)
        )
        source = row * (SIDE + 2) + col
        total = jnp.zeros((16, 256), F32)
        for half in range(2):
            part = slice(128 * half, 128 * half + 128)
            kern = lax.rsqrt(mm(flipped[source, part, :48], feature))
            high = kern.astype(BF16)
            low = (kern - high.astype(F32)).astype(BF16)
            weights = jnp.concatenate([high, low], 0)
            total = total + mm(jnp.concatenate([vec[:, part]] * 2, 1), weights)
        return total

    def own_rows(t):
        outer = t // 3
        i = outer * 3 * rep_at + (1 - outer) * (1 + rep_at)
        row = outer * (1 + 2 * rep_at + t - 3) + (1 - outer) * (1 + rep_at + t)
        step = (outer + 1 + rep_at) % 2
        return i, row, step

    for k in range(2):
        for j in range(SIDE):
            sums[k, j] = jnp.zeros((16, 256), F32)

    def own_pairs(t, carry):
        i, row, step = own_rows(t)
        for j in range(SIDE):
            total = sums[step, j]
            for col in range(max(j, 1), min(j + 3, SIDE + 1)):
                total = total + pair(i, j, row, col)
            sums[step, j] = total
        return carry

    lax.fori_loop(0, 5, own_pairs, 0)
    halo_wait(pack_copies)
    for j in range(SIDE + 2):
        flip(5 * rep_at, j)
    for k in range(3):
        flip(1 + rep_at + k, 0)
        flip(1 + rep_at + k, SIDE + 1)

    def side_pairs(t, carry):
        i, row, step = own_rows(t)
        sums[step, 0] += pair(i, 0, row, 0)
        sums[step, SIDE - 1] += pair(i, SIDE - 1, row, SIDE + 1)
        return carry

    lax.fori_loop(0, 5, side_pairs, 0)
    for j in range(SIDE):
        total = sums[rep_at, j]
        for col in range(j, j + 3):
            total = total + pair(3 * rep_at, j, 5 * rep_at, col)
        sums[rep_at, j] = total

    def near_copy(row, step):
        at = pl.ds(SIDE * row, SIDE)
        return pltpu.make_async_remote_copy(
            src_ref=near_out.at[at],
            dst_ref=near.at[at],
            send_sem=near_send.at[step],
            recv_sem=near_recv.at[step],
            device_id={"rep": 1 - rep_at},
            device_id_type=MESH,
        )

    for step in range(2):
        row = 2 * rep_at + step
        for j in range(SIDE):
            total = sums[step, j]
            result = QUAD_WEIGHT * (total[0:8] + total[8:16])
            near[SIDE * row + j] = result[0:4]
            near_out[SIDE * row + j] = result[4:8]
        near_copy(row, step).start()

    def spread_wait(step, carry):
        spread_copy(step, True).wait_send()
        spread_copy(step, False).wait_recv()
        return carry

    lax.fori_loop(1, count, spread_wait, 0)

    def padded_read(row, col):
        row_ok = (row >= 0) & (row < leaf_total)
        col_ok = (col >= 0) & (col < sub_total)
        at = jnp.clip(row, 0, leaf_total - 1) * sub_total + jnp.clip(col, 0, sub_total - 1)
        return jnp.where(row_ok & col_ok, gathered[at], 0.0)

    for copy in coarse_copies:
        copy.wait()
    current = gathered[...].reshape(count * 8, 256)
    rows_here, cols_here = leaf_total, sub_total
    coarse_local = []
    for pos in range(coarse_levels):
        raised = mm_split(current, up_ref[0], up_ref[1])
        p_rows, p_cols = rows_here // 2, cols_here // 2
        for a in range(p_rows + 2):
            for b in range(p_cols + 2):
                if a in (0, p_rows + 1) or b in (0, p_cols + 1):
                    level_mom[pos, a, b] = empty
        tiles = []
        for a in range(p_rows):
            for b in range(p_cols):
                kids = []
                for d in range(2):
                    for e in range(2):
                        at = 8 * ((2 * a + d) * cols_here + 2 * b + e)
                        kids.append(raised[at : at + 8])
                tile = jnp.concatenate(kids, 1)
                level_mom[pos, a + 1, b + 1] = tile
                tiles.append(tile)
        pi = leaf_at // 2 ** (pos + 1)
        pj = sub_at // 2 ** (pos + 1)
        window = jnp.concatenate(
            [level_mom[pos, pi + a, pj + b] for a in range(3) for b in range(3)], 1
        )
        got = mm(rows_of_halves(window), coarse_w[pos])
        coarse_local.append(got[0:8, 0:64] + got[8:16, 0:64] + got[0:8, 64:128])
        current = jnp.concatenate(tiles, 0)
        rows_here, cols_here = p_rows, p_cols

    summed = coarse_local[-1]
    for pos in range(coarse_levels - 1, 0, -1):
        children = mm_split(summed, down_ref[0], down_ref[1])
        row_bit = lax.rem(leaf_at // 2 ** (pos - 1), 2)
        col_bit = lax.rem(sub_at // 2 ** (pos - 1), 2)
        child = 2 * row_bit + col_bit
        summed = coarse_local[pos - 1]
        for k in range(4):
            summed = summed + jnp.where(child == k, children[:, 64 * k : 64 * k + 64], 0.0)

    halo_wait(mom_copies)
    fine_copy.wait()
    window = jnp.concatenate(
        [padded_read(leaf_at + a, sub_at + b) for a in (-1, 0, 1) for b in (-1, 0, 1)], 1
    )
    level_one = mm_split(summed, down_ref[0], down_ref[1]) + mm_split(
        window, fine_w[1, 0], fine_w[1, 1]
    )
    stacked = jnp.concatenate([level_one[:, 64 * k : 64 * k + 64] for k in range(4)], 0)
    window = jnp.concatenate(
        [
            jnp.concatenate([mom[a + di, b + dj] for a in range(2) for b in range(2)], 0)
            for di in range(3)
            for dj in range(3)
        ],
        1,
    )
    level_zero = mm_split(stacked, down_ref[0], down_ref[1]) + mm_split(
        window, fine_w[0, 0], fine_w[0, 1]
    )
    for step in range(2):
        near_copy(2 * rep_at + step, step).wait_send()
        near_copy(2 - 2 * rep_at + step, step).wait_recv()
    for i in range(SIDE):
        for j in range(SIDE):
            row = 8 * (2 * (i // 2) + j // 2)
            at = 64 * (2 * (i % 2) + j % 2)
            coef = level_zero[row : row + 8, at : at + 64]
            high, low = halves(coef)
            wide = basis[i * SIDE + j]
            left = jnp.concatenate([high, low], 0).astype(BF16)
            got = mm(left, wide[:64])
            got_low = mm(left, wide[64:])
            result = near[i * SIDE + j] + got[0:4] + got[8:12] + got_low[0:4]
            for c in range(4):
                out_ref[c, i, j : j + 1] = result[c : c + 1]


def local(coords, vector):
    leaf_total = lax.axis_size("leaf")
    sub_total = lax.axis_size("sub")
    count = leaf_total * sub_total
    top_level = (SIDE * sub_total).bit_length() - 1
    coarse_levels = top_level - 2

    nodes = np.array(poly_values(CHEB_NODES))
    index = np.arange(16)
    node_table = np.concatenate([nodes[:, index // 4], nodes[:, index % 4]], 0)
    node_table = np.repeat(node_table[:, :, None], 256, 2).astype(np.float32)
    table = transfer_table()
    up = np.stack(halves_numpy(table.reshape(256, 64)))
    down = np.stack(halves_numpy(table.reshape(256, 64).T))
    fine = np.stack([np.stack(halves_numpy(parent_couplings(level))) for level in range(2)])
    coarse = []
    for level in range(2, top_level):
        high, low = halves_numpy(parent_couplings(level))
        high = high.reshape(2304, 4, 64).transpose(1, 0, 2)
        low = low.reshape(2304, 4, 64).transpose(1, 0, 2)
        coarse.append(np.concatenate([high, low], 2))
    coarse = np.stack(coarse)

    vmem = pl.BlockSpec(memory_space=pltpu.VMEM)
    hbm = pl.BlockSpec(memory_space=pltpu.HBM)
    dma = pltpu.SemaphoreType.DMA
    return pl.pallas_call(
        functools.partial(body, leaf_total, sub_total, coarse_levels),
        out_shape=jax.ShapeDtypeStruct(vector.shape, F32),
        in_specs=[hbm] * 7,
        out_specs=vmem,
        scratch_shapes=[
            pltpu.VMEM(coords.shape, F32),
            pltpu.VMEM(vector.shape, F32),
            pltpu.VMEM(node_table.shape, F32),
            pltpu.VMEM(up.shape, BF16),
            pltpu.VMEM(down.shape, BF16),
            pltpu.VMEM((2, SIDE + 2, SIDE + 2, 8, 256), F32),
            pltpu.VMEM((SIDE * SIDE, 128, 256), BF16),
            pltpu.VMEM(((SIDE + 2) ** 2, 256, 128), BF16),
            pltpu.VMEM((SIDE * SIDE, 4, 256), F32),
            pltpu.VMEM((SIDE * SIDE, 4, 256), F32),
            pltpu.VMEM((2, SIDE, 16, 256), F32),
            pltpu.VMEM((4, 4, 8, 256), F32),
            pltpu.VMEM((count, 8, 256), F32),
            pltpu.VMEM((coarse_levels, leaf_total // 2 + 2, sub_total // 2 + 2, 8, 256), F32),
            pltpu.VMEM((2, 2, 2304, 256), BF16),
            pltpu.VMEM((coarse_levels, 2304, 128), BF16),
            dma((5,)),
            dma,
            dma((coarse_levels,)),
            dma((8, 2)),
            dma((8, 2)),
            dma((8,)),
            dma((8,)),
            dma((count,)),
            dma((count,)),
            dma,
            dma,
            dma((2,)),
            dma((2,)),
        ],
        compiler_params=pltpu.CompilerParams(
            collective_id=0, has_side_effects=True, vmem_limit_bytes=60 * 1024 * 1024
        ),
    )(coords, vector, node_table, up, down, fine, coarse)


def solution(mesh):
    placed = (P(None, ("groups", "leaf"), "sub", None), P("rep", ("groups", "leaf"), "sub", None))
    return jax.shard_map(
        local,
        mesh=mesh,
        in_specs=placed,
        out_specs=P("rep", ("groups", "leaf"), "sub", None),
        check_vma=False,
    )
```
